32 devices in a mesh: ctx: 16 (over z, y, core), tp: 2 (over x).
Axes of the slice: x: 2, y: 2, z: 4, core: 2. Of those that a mesh axis runs over, the one named last changes fastest.
Arguments:
- queries: bfloat16 [2048, 2048], P('ctx', 'tp'), may hold values from -6 to 6
- keys_values: bfloat16 [2048, 256], P('ctx', 'tp'), may hold values from -6 to 6
- forward_out: bfloat16 [2048, 2048], P('ctx', 'tp'), may hold values from -6 to 6
- out_grad: bfloat16 [2048, 2048], P('ctx', 'tp'), may hold values from -6 to 6
- kv_weight: bfloat16 [14848, 256], P(None, 'tp'), may hold values from -3 to 3
- span_table: int32 [32], replicated, may hold values from 0 to 31, each once
Outputs:
- query_grad: bfloat16 [2048, 2048], P('ctx', 'tp')
- input_grad: bfloat16 [2048, 14848], P('ctx', 'tp')
The draws below stay inside these ranges and needn't reach their ends.
Inputs may be any that keep to these rules, and one draw needn't show every extreme that they name: `span_table`: a permutation: every sequence block appears once.
All inputs are finite; a program needn't handle non-finite values.
Results may differ from the reference program's by a relative error of at most 0.0057.
Values may be sent and summed in bfloat16 or wider, within the bound.
A program may use at most 64 MiB of HBM per device.

```python
import jax
import jax.numpy as jnp
from jax import lax

D = 14848
HEAD = 64
HG = 16
KV = 2
HEADS = 32
SEQ = 2048
SPAN = 64
SPANS = 32
KBLOCK = 512


def draw_queries(key, part):
    key = jax.random.fold_in(key, 1)
    return jnp.clip(jax.random.normal(key, (SEQ, HEADS * HEAD)), -4.0, 4.0).astype(jnp.bfloat16)


def draw_keys_values(key, part):
    key = jax.random.fold_in(key, 3)
    return jnp.clip(jax.random.normal(key, (SEQ, KV * 2 * HEAD)), -4.0, 4.0).astype(jnp.bfloat16)


def steps_of(rng, dims, cuts, low, top_value):
    def one(dim, parts):
        heights = jax.random.uniform(jax.random.fold_in(jax.random.fold_in(rng, 6), dim), (parts,), jnp.float32, low / len(cuts), top_value / len(cuts))
        return jnp.repeat(jnp.exp(heights), dims[dim] // parts).reshape((-1,) + (1,) * (len(dims) - dim - 1))

    loudness = one(*cuts[0])
    for cut in cuts[1:]:
        loudness = loudness * one(*cut)
    return loudness


def bell_draw(stream_key, shape, deviation, reach, pieces=(), kind=jnp.bfloat16):
    loudness = steps_of(stream_key, shape, pieces, -0.22, 0.18) if pieces else 1.0
    drawn = jax.random.normal(stream_key, shape, jnp.float32) * deviation * loudness
    return jnp.minimum(jnp.maximum(drawn, -reach), reach).astype(kind)


def setup_inputs(seed: int = 0) -> dict:
    key_of = jax.random.split(jax.random.key(seed), 7)
    return {
        "queries": draw_queries(jax.random.fold_in(key_of[6], 71), 0),
        "keys_values": draw_keys_values(jax.random.fold_in(key_of[6], 71), 0),
        "forward_out": bell_draw(key_of[2], (SEQ, HEADS * HEAD), 1.0, 6.0, ((0, 16), (1, 2))),
        "out_grad": bell_draw(key_of[3], (SEQ, HEADS * HEAD), 1.0, 6.0, ((0, 16), (1, 2))),
        "kv_weight": bell_draw(key_of[4], (D, KV * 2 * HEAD), 0.5, 3.0, ((1, 2),)),
        "span_table": jax.random.permutation(key_of[5], SPANS).astype(jnp.int32),
    }


softmax_scale = 0.125
masked_score = -1.0e30


def reference(queries, keys_values, forward_out, out_grad, kv_weight, span_table):
    row_ids = jnp.arange(SEQ, dtype=jnp.int32)
    position = (span_table[row_ids // SPAN] * SPAN + row_ids % SPAN).astype(jnp.int32)
    query_parts = []
    kv_parts = []
    for group_index in range(KV):
        low = group_index * HG * HEAD
        query_cols = queries[:, low:low + HG * HEAD].reshape(SEQ, HG, HEAD).astype(jnp.float32)
        grad_cols = out_grad[:, low:low + HG * HEAD].reshape(SEQ, HG, HEAD).astype(jnp.float32)
        forward_cols = forward_out[:, low:low + HG * HEAD].reshape(SEQ, HG, HEAD).astype(jnp.float32)
        key_low = group_index * 2 * HEAD
        key_cols = keys_values[:, key_low:key_low + HEAD].astype(jnp.float32)
        value_cols = keys_values[:, key_low + HEAD:key_low + 2 * HEAD].astype(jnp.float32)
        grad_dot = jnp.sum(grad_cols * forward_cols, axis=2)

        def one_block(running, block_index):
            key_sum, value_sum = running
            first_row = (block_index * KBLOCK).astype(jnp.int32)
            query_block = lax.dynamic_slice_in_dim(query_cols, first_row, KBLOCK, 0)
            grad_block = lax.dynamic_slice_in_dim(grad_cols, first_row, KBLOCK, 0)
            dot_block = lax.dynamic_slice_in_dim(grad_dot, first_row, KBLOCK, 0)
            query_pos = lax.dynamic_slice_in_dim(position, first_row, KBLOCK, 0)
            visible = (position[None, :] <= query_pos[:, None])[None]
            scores = jnp.einsum("qhd,kd->hqk", query_block, key_cols) * softmax_scale
            scores = jnp.where(visible, scores, masked_score)
            row_top = jnp.max(scores, axis=2)
            row_total = jnp.sum(jnp.where(visible, jnp.exp(scores - row_top[:, :, None]), 0.0), axis=2)
            lse = row_top + jnp.log(row_total)
            probs = jnp.where(visible, jnp.exp(scores - lse[:, :, None]), 0.0)
            weights = probs.astype(jnp.bfloat16).astype(jnp.float32)
            dprobs = jnp.einsum("qhd,kd->hqk", grad_block, value_cols)
            dscores = (probs * (dprobs - dot_block.T[:, :, None])).astype(jnp.bfloat16).astype(jnp.float32)
            query_grad = (jnp.einsum("hqk,kd->qhd", dscores, key_cols) * softmax_scale).astype(jnp.bfloat16)
            key_sum = key_sum + jnp.einsum("hqk,qhd->kd", dscores, query_block) * softmax_scale
            value_sum = value_sum + jnp.einsum("hqk,qhd->kd", weights, grad_block)
            return (key_sum, value_sum), query_grad

        start = (jnp.zeros((SEQ, HEAD), jnp.float32), jnp.zeros((SEQ, HEAD), jnp.float32))
        (key_sum, value_sum), query_blocks = lax.scan(one_block, start, jnp.arange(SEQ // KBLOCK, dtype=jnp.int32))
        query_parts.append(query_blocks.reshape(SEQ, HG * HEAD))
        kv_parts.append(key_sum.astype(jnp.bfloat16))
        kv_parts.append(value_sum.astype(jnp.bfloat16))
    query_grad = jnp.concatenate(query_parts, axis=1)
    kv_grad = jnp.concatenate(kv_parts, axis=1)
    input_grad = lax.dot_general(kv_grad, kv_weight, (((1,), (1,)), ((), ())), preferred_element_type=jnp.float32)
    return query_grad, input_grad.astype(jnp.bfloat16)
```

```python
import jax
import jax.numpy as jnp
from jax import lax
from jax.experimental import pallas as pl
from jax.experimental.pallas import tpu as pltpu
from jax.sharding import PartitionSpec as P

HEAD = 64
CHUNK_HEADS = 8
KEY_TILE = 256
softmax_scale = 0.125
log2_e = 1.4426950408889634
hidden = -1e30

NT = (((1,), (1,)), ((), ()))
NN = (((1,), (0,)), ((), ()))


def dot(a, b, dims=NN):
    return lax.dot_general(a, b, dims, preferred_element_type=jnp.float32)


def spread_queries(table_ref, first_span, half, q_ref, do_ref, fo_ref, qx, qs, dox):
    span_rows = q_ref.shape[0] // 2
    heads = q_ref.shape[1] // HEAD
    span = table_ref[first_span + half]
    row = lax.broadcasted_iota(jnp.int32, (span_rows, 2 * HEAD), 0)
    col = lax.broadcasted_iota(jnp.int32, (span_rows, 2 * HEAD), 1)
    blocked = jnp.where(col < HEAD, col - row, col - HEAD - span) > 0
    mask_cols = jnp.where(blocked, hidden, 0.0).astype(jnp.bfloat16)
    lane = lax.broadcasted_iota(jnp.int32, (span_rows, HEAD), 1)
    rows = pl.ds(half * span_rows, span_rows)
    for head in range(heads):
        pair = pl.ds(head // 2 * 2 * HEAD, 2 * HEAD)
        low = head % 2 * HEAD
        at = pl.ds((half * heads + head) * span_rows, span_rows)
        query = q_ref[rows, pair].astype(jnp.float32)[:, low:low + HEAD]
        grad = do_ref[rows, pair].astype(jnp.float32)[:, low:low + HEAD]
        forward = fo_ref[rows, pair].astype(jnp.float32)[:, low:low + HEAD]
        scaled = query * (softmax_scale * log2_e)
        top = scaled.astype(jnp.bfloat16).astype(jnp.float32)
        qx[at, 0:2 * HEAD] = jnp.concatenate([top, scaled - top], axis=1).astype(jnp.bfloat16)
        qx[at, 2 * HEAD:4 * HEAD] = mask_cols
        qs[at, :] = query.astype(jnp.bfloat16)
        left = -jnp.sum(grad * forward, axis=1, keepdims=True)
        tail = jnp.zeros((span_rows, HEAD), jnp.float32)
        for place in range(3):
            part = left.astype(jnp.bfloat16).astype(jnp.float32)
            tail = jnp.where(lane == place, part, tail)
            left = left - part
        dox[at, :] = jnp.concatenate([grad, tail], axis=1).astype(jnp.bfloat16)


def spread_keys(table_ref, first_span, first_row, block, kx, kt, vx):
    rows = block.shape[0]
    span_rows = rows // 2
    wide = block.astype(jnp.float32)
    key, value = wide[:, :HEAD], wide[:, HEAD:]
    lane = lax.broadcasted_iota(jnp.int32, (rows, HEAD), 1)
    ones = jnp.where(lane < 3, 1.0, 0.0)
    at = pl.ds(first_row, rows)
    vx[at, :] = jnp.concatenate([value, ones], axis=1).astype(jnp.bfloat16)
    eye = (
        lax.broadcasted_iota(jnp.int32, (HEAD, HEAD), 0)
        == lax.broadcasted_iota(jnp.int32, (HEAD, HEAD), 1)
    ).astype(jnp.bfloat16)
    kt[:, at] = dot(eye, key.astype(jnp.bfloat16), NT).astype(jnp.bfloat16)
    twice = jnp.concatenate([key, key], axis=1).astype(jnp.bfloat16)
    row = lax.broadcasted_iota(jnp.int32, (rows, 2 * HEAD), 0)
    col = lax.broadcasted_iota(jnp.int32, (rows, 2 * HEAD), 1)
    span_index = first_row // span_rows
    span = jnp.where(row < span_rows, table_ref[span_index], table_ref[span_index + 1])
    inner = jnp.where(row < span_rows, row, row - span_rows)
    for half in range(2):
        own = table_ref[first_span + half]
        wanted = jnp.where(col < HEAD, jnp.where(span == own, inner, -1), span + HEAD)
        kx[half, at, 0:2 * HEAD] = twice
        kx[half, at, 2 * HEAD:4 * HEAD] = jnp.where(wanted == col, 1.0, 0.0).astype(jnp.bfloat16)


def attention(chunk_count, chunk_rows, total_rows, span_rows, kx, kt, vx, qx, qs, dox, score, dk, dv, dq_ref):
    tiles = total_rows // KEY_TILE
    heads = dq_ref.shape[1] // HEAD

    def chunk_at(chunk):
        return pl.ds(chunk * chunk_rows, chunk_rows)

    def score_tile(chunk, tile, top):
        at = pl.ds(tile * KEY_TILE, KEY_TILE)
        half = chunk * 2 // chunk_count
        s = dot(kx[half, at, :], qx[chunk_at(chunk), :], NT)
        score[chunk % 2, at, :] = s
        return jnp.maximum(top, jnp.max(s.reshape(KEY_TILE // 8, 8, chunk_rows), axis=0))

    def exp_tile(chunk, tile, peak, total):
        at = pl.ds(tile * KEY_TILE, KEY_TILE)
        e = jnp.exp2(score[chunk % 2, at, :] - peak)
        score[chunk % 2, at, :] = e
        return total + jnp.sum(e.reshape(KEY_TILE // 8, 8, chunk_rows), axis=0)

    top_start = jnp.full((8, chunk_rows), hidden, jnp.float32)
    zero = jnp.zeros((8, chunk_rows), jnp.float32)
    top = lax.fori_loop(0, tiles, lambda tile, top: score_tile(0, tile, top), top_start)
    for chunk in range(chunk_count):
        peak = jnp.max(top, axis=0, keepdims=True)

        def first(tile, running, chunk=chunk, peak=peak):
            top, total = running
            if chunk + 1 < chunk_count:
                top = score_tile(chunk + 1, tile, top)
            return top, exp_tile(chunk, tile, peak, total)

        top, total = lax.fori_loop(0, tiles, first, (top_start, zero))
        inverse = 1.0 / jnp.sum(total, axis=0, keepdims=True)

        def second(tile, dqt, chunk=chunk, inverse=inverse):
            at = pl.ds(pl.multiple_of(tile * KEY_TILE, KEY_TILE), KEY_TILE)
            probs = score[chunk % 2, at, :] * inverse
            dprobs = dot(vx[at, :], dox[chunk_at(chunk), :], NT)
            dscores = (probs * dprobs).astype(jnp.bfloat16)
            dv_add = dot(probs.astype(jnp.bfloat16), dox[chunk_at(chunk), :])[:, :HEAD]
            dk_add = dot(dscores, qs[chunk_at(chunk), :])
            if chunk == 0:
                dv[at, :] = dv_add
                dk[at, :] = dk_add
            else:
                dv[at, :] += dv_add
                dk[at, :] += dk_add
            return dqt + dot(kt[:, at], dscores)

        dqt = lax.fori_loop(0, tiles, second, jnp.zeros((HEAD, chunk_rows), jnp.float32))
        dq = (dqt * softmax_scale).T
        half = chunk * 2 // chunk_count
        first_head = chunk * CHUNK_HEADS % heads
        for pair in range(CHUNK_HEADS // 2):
            parts = [
                dq[(2 * pair + side) * span_rows:(2 * pair + side + 1) * span_rows, :]
                for side in range(2)
            ]
            dq_ref[
                pl.ds(half * span_rows, span_rows),
                pl.ds((first_head + 2 * pair) * HEAD, 2 * HEAD),
            ] = jnp.concatenate(parts, axis=1).astype(jnp.bfloat16)


def attention_kernel(table_ref, q_ref, do_ref, fo_ref, kv_ref, dq_ref, dkv_ref, qx, qs, dox, kx, kt, vx, score, dk, dv):
    tokens = q_ref.shape[0]
    total_rows = kv_ref.shape[0]
    first_span = lax.axis_index("ctx") * 2
    for half in range(2):
        spread_queries(table_ref, first_span, half, q_ref, do_ref, fo_ref, qx, qs, dox)

    @pl.loop(0, total_rows // tokens)
    def _(owner):
        first_row = pl.multiple_of(owner * tokens, tokens)
        spread_keys(table_ref, first_span, first_row, kv_ref[pl.ds(first_row, tokens), :], kx, kt, vx)

    chunk_rows = CHUNK_HEADS * tokens // 2
    chunk_count = qx.shape[0] // chunk_rows
    attention(chunk_count, chunk_rows, total_rows, tokens // 2, kx, kt, vx, qx, qs, dox, score, dk, dv, dq_ref)
    dkv_ref[...] = jnp.concatenate([dk[...] * softmax_scale, dv[...]], axis=1)


def attention_scratch(tokens, heads, total_rows):
    rows = tokens * heads
    chunk_rows = CHUNK_HEADS * tokens // 2
    return [
        pltpu.VMEM((rows, 4 * HEAD), jnp.bfloat16),
        pltpu.VMEM((rows, HEAD), jnp.bfloat16),
        pltpu.VMEM((rows, 2 * HEAD), jnp.bfloat16),
        pltpu.VMEM((2, total_rows, 4 * HEAD), jnp.bfloat16),
        pltpu.VMEM((HEAD, total_rows), jnp.bfloat16),
        pltpu.VMEM((total_rows, 2 * HEAD), jnp.bfloat16),
        pltpu.VMEM((2, total_rows, chunk_rows), jnp.float32),
        pltpu.VMEM((total_rows, HEAD), jnp.float32),
        pltpu.VMEM((total_rows, HEAD), jnp.float32),
    ]


def on_device(queries, keys_values, forward_out, out_grad, kv_weight, span_table):
    tokens = queries.shape[0]
    heads = queries.shape[1] // HEAD
    tp_size = lax.axis_size("tp")
    ctx_size = lax.axis_size("ctx")
    tp_index = lax.axis_index("tp")
    core = lax.axis_index("ctx") % 2
    total_rows = tokens * ctx_size
    features = kv_weight.shape[0] // tp_size
    share = features // 2
    weights = []
    for step in range(1, tp_size):
        target = (tp_index + step) % tp_size
        piece = lax.dynamic_slice_in_dim(kv_weight, target * features + core * share, share, 0)
        mine = lax.ppermute(piece, "tp", [(s, (s + step) % tp_size) for s in range(tp_size)])
        mate = lax.ppermute(mine, "ctx", [(s, s ^ 1) for s in range(ctx_size)])
        low = jnp.where(core == 0, mine, mate)
        high = jnp.where(core == 0, mate, mine)
        weights.append(jnp.concatenate([low, high], axis=0))
    gathered = lax.all_gather(keys_values, "ctx", axis=0, tiled=True)
    vmem = pl.BlockSpec(memory_space=pltpu.VMEM)
    query_grad, kv_terms = pl.pallas_call(
        attention_kernel,
        out_shape=(
            jax.ShapeDtypeStruct(queries.shape, jnp.bfloat16),
            jax.ShapeDtypeStruct((total_rows, 2 * HEAD), jnp.float32),
        ),
        in_specs=[pl.BlockSpec(memory_space=pltpu.SMEM)] + [vmem] * 4,
        out_specs=(vmem, vmem),
        scratch_shapes=attention_scratch(tokens, heads, total_rows),
        compiler_params=pltpu.CompilerParams(vmem_limit_bytes=56 * 2**20),
        cost_estimate=pl.CostEstimate(
            flops=10 * tokens * heads * total_rows * 4 * HEAD, bytes_accessed=4 * 2**20, transcendentals=0
        ),
    )(span_table, queries, out_grad, forward_out, gathered)
    kv_grad = lax.psum_scatter(kv_terms, "ctx", scatter_dimension=0, tiled=True).astype(jnp.bfloat16)
    own = lax.dynamic_slice_in_dim(kv_weight, tp_index * features, features, 0)
    total = dot(kv_grad, own, NT)
    for step in range(1, tp_size):
        other = lax.ppermute(kv_grad, "tp", [(s, (s + step) % tp_size) for s in range(tp_size)])
        total = total + dot(other, weights[step - 1], NT)
    return (query_grad, total.astype(jnp.bfloat16))


def solution(mesh):
    placed = (P("ctx", "tp"), P("ctx", "tp"), P("ctx", "tp"), P("ctx", "tp"), P(None, "tp"), P())
    return jax.shard_map(
        on_device,
        mesh=mesh,
        in_specs=placed,
        out_specs=(P("ctx", "tp"), P("ctx", "tp")),
        check_vma=False,
    )
```

```python
import functools

import jax
import jax.numpy as jnp
from jax import lax
from jax.experimental import pallas as pl
from jax.experimental.pallas import tpu as pltpu
from jax.sharding import PartitionSpec as P

HEAD = 64
CHUNK_HEADS = 8
KEY_TILE = 256
softmax_scale = 0.125
log2_e = 1.4426950408889634
hidden = -1e30

NT = (((1,), (1,)), ((), ()))
NN = (((1,), (0,)), ((), ()))


def dot(a, b, dims=NN):
    return lax.dot_general(a, b, dims, preferred_element_type=jnp.float32)


def spread_queries(table_ref, first_span, half, q_ref, do_ref, fo_ref, qx, qs, dox, dos):
    span_rows = q_ref.shape[0] // 2
    heads = q_ref.shape[1] // HEAD
    span = table_ref[first_span + half]
    row = lax.broadcasted_iota(jnp.int32, (span_rows, 2 * HEAD), 0)
    col = lax.broadcasted_iota(jnp.int32, (span_rows, 2 * HEAD), 1)
    blocked = jnp.where(col < HEAD, col - row, col - HEAD - span) > 0
    mask_cols = jnp.where(blocked, hidden, 0.0).astype(jnp.bfloat16)
    lane = lax.broadcasted_iota(jnp.int32, (span_rows, HEAD), 1)
    rows = pl.ds(half * span_rows, span_rows)
    for head in range(heads):
        pair = pl.ds(head // 2 * 2 * HEAD, 2 * HEAD)
        low = head % 2 * HEAD
        at = pl.ds((half * heads + head) * span_rows, span_rows)
        query = q_ref[rows, pair].astype(jnp.float32)[:, low:low + HEAD]
        grad = do_ref[rows, pair].astype(jnp.float32)[:, low:low + HEAD]
        forward = fo_ref[rows, pair].astype(jnp.float32)[:, low:low + HEAD]
        scaled = query * (softmax_scale * log2_e)
        top = scaled.astype(jnp.bfloat16).astype(jnp.float32)
        qx[at, 0:2 * HEAD] = jnp.concatenate([top, scaled - top], axis=1).astype(jnp.bfloat16)
        qx[at, 2 * HEAD:4 * HEAD] = mask_cols
        blank = jnp.zeros((span_rows, HEAD), jnp.float32)
        qs[at, :] = jnp.concatenate([query * softmax_scale, blank], axis=1).astype(jnp.bfloat16)
        dos[at, :] = jnp.concatenate([blank, grad], axis=1).astype(jnp.bfloat16)
        left = -jnp.sum(grad * forward, axis=1, keepdims=True)
        tail = jnp.zeros((span_rows, HEAD), jnp.float32)
        for place in range(3):
            part = left.astype(jnp.bfloat16).astype(jnp.float32)
            tail = jnp.where(lane == place, part, tail)
            left = left - part
        dox[at, :] = jnp.concatenate([grad, tail], axis=1).astype(jnp.bfloat16)


def spread_keys(table_ref, first_span, first_row, block, kx, kt, vx):
    rows = block.shape[0]
    span_rows = rows // 2
    wide = block.astype(jnp.float32)
    key, value = wide[:, :HEAD], wide[:, HEAD:]
    lane = lax.broadcasted_iota(jnp.int32, (rows, HEAD), 1)
    ones = jnp.where(lane < 3, 1.0, 0.0)
    at = pl.ds(first_row, rows)
    vx[at, :] = jnp.concatenate([value, ones], axis=1).astype(jnp.bfloat16)
    eye = (
        lax.broadcasted_iota(jnp.int32, (HEAD, HEAD), 0)
        == lax.broadcasted_iota(jnp.int32, (HEAD, HEAD), 1)
    ).astype(jnp.bfloat16)
    kt[:, at] = dot(eye, key.astype(jnp.bfloat16), NT).astype(jnp.bfloat16)
    twice = jnp.concatenate([key, key], axis=1).astype(jnp.bfloat16)
    row = lax.broadcasted_iota(jnp.int32, (rows, 2 * HEAD), 0)
    col = lax.broadcasted_iota(jnp.int32, (rows, 2 * HEAD), 1)
    span_index = first_row // span_rows
    span = jnp.where(row < span_rows, table_ref[span_index], table_ref[span_index + 1])
    inner = jnp.where(row < span_rows, row, row - span_rows)
    for half in range(2):
        own = table_ref[first_span + half]
        wanted = jnp.where(col < HEAD, jnp.where(span == own, inner, -1), span + HEAD)
        kx[half, at, 0:2 * HEAD] = twice
        kx[half, at, 2 * HEAD:4 * HEAD] = jnp.where(wanted == col, 1.0, 0.0).astype(jnp.bfloat16)


def attention(chunk_count, chunk_rows, total_rows, span_rows, kx, kt, vx, qx, qs, dox, dos, score, dkv, dq_ref, after_chunk, tile_order, after_tile):
    tiles = total_rows // KEY_TILE
    heads = dq_ref.shape[1] // HEAD

    def chunk_at(chunk):
        return pl.ds(chunk * chunk_rows, chunk_rows)

    def tile_at(tile):
        return pl.ds(pl.multiple_of(tile * KEY_TILE, KEY_TILE), KEY_TILE)

    def score_tile(chunk, tile, top):
        half = chunk * 2 // chunk_count
        s = dot(kx[half, tile_at(tile), :], qx[chunk_at(chunk), :], NT)
        score[chunk % 2, tile_at(tile), :] = s
        return jnp.maximum(top, jnp.max(s.reshape(KEY_TILE // 8, 8, chunk_rows), axis=0))

    def exp_tile(chunk, tile, peak, total):
        e = jnp.exp2(score[chunk % 2, tile_at(tile), :] - peak)
        score[chunk % 2, tile_at(tile), :] = e
        return total + jnp.sum(e.reshape(KEY_TILE // 8, 8, chunk_rows), axis=0)

    top_start = jnp.full((8, chunk_rows), hidden, jnp.float32)
    zero = jnp.zeros((8, chunk_rows), jnp.float32)
    top = lax.fori_loop(0, tiles, lambda tile, top: score_tile(0, tile, top), top_start)
    for chunk in range(chunk_count):
        peak = jnp.max(top, axis=0, keepdims=True)

        def first(tile, running, chunk=chunk, peak=peak):
            top, total = running
            if chunk + 1 < chunk_count:
                top = score_tile(chunk + 1, tile, top)
            return top, exp_tile(chunk, tile, peak, total)

        top, total = lax.fori_loop(0, tiles, first, (top_start, zero))
        inverse = 1.0 / jnp.sum(total, axis=0, keepdims=True)

        def second(tile, dqt, chunk=chunk, inverse=inverse):
            at = tile_at(tile)
            probs = score[chunk % 2, at, :] * inverse
            dprobs = dot(vx[at, :], dox[chunk_at(chunk), :], NT)
            dscores = (probs * dprobs).astype(jnp.bfloat16)
            add = dot(probs.astype(jnp.bfloat16), dos[chunk_at(chunk), :])
            add = add + dot(dscores, qs[chunk_at(chunk), :])
            if chunk == 0:
                dkv[at, :] = add
            else:
                dkv[at, :] += add
            return dqt + dot(kt[:, at], dscores)

        dqt = jnp.zeros((HEAD, chunk_rows), jnp.float32)
        if chunk + 1 < chunk_count:
            dqt = lax.fori_loop(0, tiles, second, dqt)
        else:
            for turn in range(tiles):
                dqt = second(tile_order(turn), dqt)
                after_tile(turn)
        dq = (dqt * softmax_scale).T
        half = chunk * 2 // chunk_count
        first_head = chunk * CHUNK_HEADS % heads
        for pair in range(CHUNK_HEADS // 2):
            parts = [
                dq[(2 * pair + side) * span_rows:(2 * pair + side + 1) * span_rows, :]
                for side in range(2)
            ]
            dq_ref[
                pl.ds(half * span_rows, span_rows),
                pl.ds((first_head + 2 * pair) * HEAD, 2 * HEAD),
            ] = jnp.concatenate(parts, axis=1).astype(jnp.bfloat16)
        after_chunk(chunk)


def weight_pieces(share, most):
    return next(count for count in (4, 2, 1) if count <= most and share % (16 * count) == 0)


def backward_kernel(
    ctx_size, tp_size,
    table_ref, q_ref, do_ref, fo_ref, kv_ref, w_ref,
    dq_ref, grad_ref, wall_ref,
    qx, qs, dox, dos, kx, kt, vx, score, dkv,
    gathered, mate_sum, row_out, row_in, far_out, far_in,
    gz_send, gz_recv, gy_send, gy_recv, gm_send, gm_recv,
    rm_send, rm_recv, ry_send, ry_recv, rz_send, rz_recv,
    wx_send, wx_recv, wm_send, wm_recv, own_sem, t_send, t_recv,
):
    tokens = q_ref.shape[0]
    total_rows = gathered.shape[0]
    far = ctx_size // 4
    me = lax.axis_index("ctx")
    tp = lax.axis_index("tp")
    hi, mid, core = me // 4, lax.rem(me // 2, 2), lax.rem(me, 2)

    def place(h, m, k):
        return h * 4 + m * 2 + k

    def around(step):
        return lax.rem(hi + step, far)

    def behind(step):
        return lax.rem(hi + far - step, far)

    def block(owner):
        return gathered.at[pl.ds(pl.multiple_of(owner * tokens, tokens), tokens), :]

    def send(src, dst, send_sem, recv_sem, axis, target):
        copy = pltpu.make_async_remote_copy(
            src_ref=src, dst_ref=dst, send_sem=send_sem, recv_sem=recv_sem,
            device_id={axis: target}, device_id_type=pl.DeviceIdType.MESH,
        )
        copy.start()
        return copy

    row_mate, core_mate = place(hi, 1 - mid, core), place(hi, mid, 1 - core)
    partners = [("ctx", place(around(step), mid, core)) for step in range(1, far)]
    partners += [("ctx", row_mate), ("ctx", core_mate)]
    partners += [("tp", lax.rem(tp + step, tp_size)) for step in range(1, tp_size)]
    barrier = pltpu.get_barrier_semaphore()
    for axis, target in partners:
        pl.semaphore_signal(barrier, inc=1, device_id={axis: target}, device_id_type=pl.DeviceIdType.MESH)
    pl.semaphore_wait(barrier, len(partners))

    waits = []
    for step in range(1, far):
        waits.append(send(kv_ref, block(me), gz_send.at[step], gz_recv.at[step], "ctx", place(around(step), mid, core)))
    from_far = list(waits)
    from_row = [send(kv_ref, block(me), gy_send.at[0], gy_recv.at[0], "ctx", row_mate)]
    from_core = [send(kv_ref, block(me), gm_send.at[0, 0], gm_recv.at[0, 0], "ctx", core_mate)]

    features = w_ref.shape[0] // tp_size
    share = features // 2
    pieces = weight_pieces(share, wx_send.shape[1])
    piece_rows = share // pieces
    own_copy = pltpu.make_async_copy(
        w_ref.at[pl.ds(pl.multiple_of(tp * features, 16), features), :], wall_ref.at[:, pl.ds(0, 2 * HEAD)], own_sem
    )
    own_copy.start()

    def wall_piece(step, side, piece):
        first = pl.multiple_of(side * share + piece * piece_rows, 16)
        return wall_ref.at[pl.ds(first, piece_rows), pl.ds(step * 2 * HEAD, 2 * HEAD)]

    weight_in = {}
    for piece in range(pieces):
        for step in range(1, tp_size):
            target = lax.rem(tp + step, tp_size)
            first = pl.multiple_of(target * features + core * share + piece * piece_rows, 16)
            weight_in[step, piece] = send(
                w_ref.at[pl.ds(first, piece_rows), :], wall_piece(step, core, piece),
                wx_send.at[step, piece], wx_recv.at[step, piece], "tp", target,
            )
    weight_mate = []

    first_span = me * 2
    spread_queries(table_ref, first_span, 0, q_ref, do_ref, fo_ref, qx, qs, dox, dos)
    for step in range(1, far):
        from_far[step - 1].wait_recv()
        here = block(place(behind(step), mid, core))
        from_row.append(send(here, here, gy_send.at[step], gy_recv.at[step], "ctx", row_mate))
        from_core.append(send(here, here, gm_send.at[step, 0], gm_recv.at[step, 0], "ctx", core_mate))
    spread_queries(table_ref, first_span, 1, q_ref, do_ref, fo_ref, qx, qs, dox, dos)
    for step in range(far):
        from_row[step].wait_recv()
        here = block(place(behind(step), 1 - mid, core))
        from_core.append(send(here, here, gm_send.at[step, 1], gm_recv.at[step, 1], "ctx", core_mate))

    def take(owner, ref):
        first_row = pl.multiple_of(owner * tokens, tokens)
        spread_keys(table_ref, first_span, first_row, ref[...], kx, kt, vx)

    take(me, kv_ref)

    @pl.loop(1, 2 * far)
    def _(turn):
        owner = place(behind(turn // 2), lax.rem(mid + lax.rem(turn, 2), 2), core)
        take(owner, block(owner))

    for copy in from_core:
        copy.wait_recv()

    @pl.loop(0, 2 * far)
    def _(turn):
        owner = place(behind(turn // 2), lax.rem(mid + lax.rem(turn, 2), 2), 1 - core)
        take(owner, block(owner))

    for copy in from_far + from_row + from_core:
        copy.wait_send()

    def after_chunk(chunk):
        if chunk < pieces:
            for step in range(1, tp_size):
                weight_in[step, chunk].wait_recv()
                here = wall_piece(step, core, chunk)
                weight_mate.append(
                    send(here, here, wm_send.at[step, chunk], wm_recv.at[step, chunk], "ctx", core_mate)
                )

    def turn_place(turn):
        return around(turn % far + 1), (1 - mid if turn < far else mid)

    def tile_order(turn):
        h, m = turn_place(turn)
        return h * 2 + m

    def part(turn, k):
        h, m = turn_place(turn)
        return pl.ds(pl.multiple_of(place(h, m, k) * tokens, tokens), tokens)

    to_core, to_row, to_far = [], [], []

    def pass_on(turn):
        to_core[turn].wait_recv()
        total = dkv[part(turn, core), :] + mate_sum[turn]
        step = turn % far
        if turn < far:
            row_out[step] = total.astype(jnp.bfloat16)
            to_row.append(send(row_out.at[step], row_in.at[step], ry_send.at[step], ry_recv.at[step], "ctx", row_mate))
            return
        to_row[step].wait_recv()
        total = total + row_in[step].astype(jnp.float32)
        if step + 1 < far:
            far_out[step] = total.astype(jnp.bfloat16)
            h, _ = turn_place(turn)
            to_far.append(
                send(far_out.at[step], far_in.at[step], rz_send.at[step], rz_recv.at[step], "ctx", place(h, mid, core))
            )
            return
        for copy in to_far:
            copy.wait_recv()
        for step in range(far - 1):
            total = total + far_in[step].astype(jnp.float32)
        grad_ref[:, 0:2 * HEAD] = total.astype(jnp.bfloat16)

    lag = 2

    def after_tile(turn):
        to_core.append(
            send(dkv.at[part(turn, 1 - core), :], mate_sum.at[turn], rm_send.at[turn], rm_recv.at[turn], "ctx", core_mate)
        )
        if turn >= lag:
            pass_on(turn - lag)

    chunk_rows = CHUNK_HEADS * tokens // 2
    chunk_count = qx.shape[0] // chunk_rows
    attention(
        chunk_count, chunk_rows, total_rows, tokens // 2, kx, kt, vx, qx, qs, dox, dos, score, dkv, dq_ref,
        after_chunk, tile_order, after_tile,
    )
    for turn in range(2 * far - lag, 2 * far):
        pass_on(turn)
    last = []
    for step in range(1, tp_size):
        last.append(
            send(
                grad_ref.at[:, pl.ds(0, 2 * HEAD)], grad_ref.at[:, pl.ds(step * 2 * HEAD, 2 * HEAD)],
                t_send.at[step], t_recv.at[step], "tp", lax.rem(tp + step, tp_size),
            )
        )
    for copy in to_core + to_row + to_far + list(weight_in.values()):
        copy.wait_send()
    for copy in weight_mate + last:
        copy.wait()
    own_copy.wait()


def scratch(tokens, heads, ctx_size, tp_size):
    total_rows = tokens * ctx_size
    rows = tokens * heads
    chunk_rows = CHUNK_HEADS * tokens // 2
    far = ctx_size // 4
    block = (tokens, 2 * HEAD)
    sems = pltpu.SemaphoreType.DMA
    return [
        pltpu.VMEM((rows, 4 * HEAD), jnp.bfloat16),
        pltpu.VMEM((rows, 2 * HEAD), jnp.bfloat16),
        pltpu.VMEM((rows, 2 * HEAD), jnp.bfloat16),
        pltpu.VMEM((rows, 2 * HEAD), jnp.bfloat16),
        pltpu.VMEM((2, total_rows, 4 * HEAD), jnp.bfloat16),
        pltpu.VMEM((HEAD, total_rows), jnp.bfloat16),
        pltpu.VMEM((total_rows, 2 * HEAD), jnp.bfloat16),
        pltpu.VMEM((2, total_rows, chunk_rows), jnp.float32),
        pltpu.VMEM((total_rows, 2 * HEAD), jnp.float32),
        pltpu.VMEM((total_rows, 2 * HEAD), jnp.bfloat16),
        pltpu.VMEM((2 * far,) + block, jnp.float32),
        pltpu.VMEM((far,) + block, jnp.bfloat16),
        pltpu.VMEM((far,) + block, jnp.bfloat16),
        pltpu.VMEM((far,) + block, jnp.bfloat16),
        pltpu.VMEM((far,) + block, jnp.bfloat16),
        sems((far,)), sems((far,)), sems((far,)), sems((far,)), sems((far, 2)), sems((far, 2)),
        sems((2 * far,)), sems((2 * far,)), sems((far,)), sems((far,)), sems((far,)), sems((far,)),
        sems((tp_size, 4)), sems((tp_size, 4)), sems((tp_size, 4)), sems((tp_size, 4)), sems(()),
        sems((tp_size,)), sems((tp_size,)),
    ]


def on_device(queries, keys_values, forward_out, out_grad, kv_weight, span_table):
    tokens = queries.shape[0]
    heads = queries.shape[1] // HEAD
    tp_size = lax.axis_size("tp")
    ctx_size = lax.axis_size("ctx")
    features = kv_weight.shape[0] // tp_size
    vmem = pl.BlockSpec(memory_space=pltpu.VMEM)
    anywhere = pl.BlockSpec(memory_space=pl.ANY)
    query_grad, kv_grad, weights = pl.pallas_call(
        functools.partial(backward_kernel, ctx_size, tp_size),
        out_shape=(
            jax.ShapeDtypeStruct(queries.shape, jnp.bfloat16),
            jax.ShapeDtypeStruct((tokens, tp_size * 2 * HEAD), jnp.bfloat16),
            jax.ShapeDtypeStruct((features, tp_size * 2 * HEAD), jnp.bfloat16),
        ),
        in_specs=[pl.BlockSpec(memory_space=pltpu.SMEM)] + [vmem] * 4 + [anywhere],
        out_specs=(vmem, vmem, anywhere),
        scratch_shapes=scratch(tokens, heads, ctx_size, tp_size),
        compiler_params=pltpu.CompilerParams(
            vmem_limit_bytes=56 * 2**20, collective_id=0, has_side_effects=True
        ),
    )(span_table, queries, out_grad, forward_out, keys_values, kv_weight)
    return (query_grad, dot(kv_grad, weights, NT).astype(jnp.bfloat16))


def solution(mesh):
    placed = (P("ctx", "tp"), P("ctx", "tp"), P("ctx", "tp"), P("ctx", "tp"), P(None, "tp"), P())
    return jax.shard_map(
        on_device,
        mesh=mesh,
        in_specs=placed,
        out_specs=(P("ctx", "tp"), P("ctx", "tp")),
        check_vma=False,
    )
```

```python
import functools

import jax
import jax.numpy as jnp
from jax import lax
from jax.experimental import pallas as pl
from jax.experimental.pallas import tpu as pltpu
from jax.sharding import PartitionSpec as P

HEAD = 64
CHUNK_HEADS = 8
KEY_TILE = 256
softmax_scale = 0.125
log2_e = 1.4426950408889634
hidden = -1e30

NT = (((1,), (1,)), ((), ()))
NN = (((1,), (0,)), ((), ()))


def dot(a, b, dims=NN):
    return lax.dot_general(a, b, dims, preferred_element_type=jnp.float32)


def spread_queries(table_ref, first_span, half, q_ref, do_ref, fo_ref, qx, qs, dox, dos):
    span_rows = q_ref.shape[0] // 2
    heads = q_ref.shape[1] // HEAD
    span = table_ref[first_span + half]
    row = lax.broadcasted_iota(jnp.int32, (span_rows, 2 * HEAD), 0)
    col = lax.broadcasted_iota(jnp.int32, (span_rows, 2 * HEAD), 1)
    blocked = jnp.where(col < HEAD, col - row, col - HEAD - span) > 0
    mask_cols = jnp.where(blocked, hidden, 0.0).astype(jnp.bfloat16)
    lane = lax.broadcasted_iota(jnp.int32, (span_rows, HEAD), 1)
    rows = pl.ds(half * span_rows, span_rows)
    for head in range(heads):
        pair = pl.ds(head // 2 * 2 * HEAD, 2 * HEAD)
        low = head % 2 * HEAD
        at = pl.ds((half * heads + head) * span_rows, span_rows)
        query = q_ref[rows, pair].astype(jnp.float32)[:, low:low + HEAD]
        grad = do_ref[rows, pair].astype(jnp.float32)[:, low:low + HEAD]
        forward = fo_ref[rows, pair].astype(jnp.float32)[:, low:low + HEAD]
        scaled = query * (softmax_scale * log2_e)
        top = scaled.astype(jnp.bfloat16).astype(jnp.float32)
        qx[at, 0:2 * HEAD] = jnp.concatenate([top, scaled - top], axis=1).astype(jnp.bfloat16)
        qx[at, 2 * HEAD:4 * HEAD] = mask_cols
        blank = jnp.zeros((span_rows, HEAD), jnp.float32)
        qs[at, :] = jnp.concatenate([query * softmax_scale, blank], axis=1).astype(jnp.bfloat16)
        dos[at, :] = jnp.concatenate([blank, grad], axis=1).astype(jnp.bfloat16)
        left = -jnp.sum(grad * forward, axis=1, keepdims=True)
        tail = jnp.zeros((span_rows, HEAD), jnp.float32)
        for place in range(3):
            part = left.astype(jnp.bfloat16).astype(jnp.float32)
            tail = jnp.where(lane == place, part, tail)
            left = left - part
        dox[at, :] = jnp.concatenate([grad, tail], axis=1).astype(jnp.bfloat16)


def spread_keys(table_ref, first_span, first_row, block, kx, kt, vx):
    rows = block.shape[0]
    span_rows = rows // 2
    wide = block.astype(jnp.float32)
    key, value = wide[:, :HEAD], wide[:, HEAD:]
    lane = lax.broadcasted_iota(jnp.int32, (rows, HEAD), 1)
    ones = jnp.where(lane < 3, 1.0, 0.0)
    at = pl.ds(first_row, rows)
    vx[at, :] = jnp.concatenate([value, ones], axis=1).astype(jnp.bfloat16)
    eye = (
        lax.broadcasted_iota(jnp.int32, (HEAD, HEAD), 0)
        == lax.broadcasted_iota(jnp.int32, (HEAD, HEAD), 1)
    ).astype(jnp.bfloat16)
    kt[:, at] = dot(eye, key.astype(jnp.bfloat16), NT).astype(jnp.bfloat16)
    twice = jnp.concatenate([key, key], axis=1).astype(jnp.bfloat16)
    row = lax.broadcasted_iota(jnp.int32, (rows, 2 * HEAD), 0)
    col = lax.broadcasted_iota(jnp.int32, (rows, 2 * HEAD), 1)
    span_index = first_row // span_rows
    span = jnp.where(row < span_rows, table_ref[span_index], table_ref[span_index + 1])
    inner = jnp.where(row < span_rows, row, row - span_rows)
    for half in range(2):
        own = table_ref[first_span + half]
        wanted = jnp.where(col < HEAD, jnp.where(span == own, inner, -1), span + HEAD)
        kx[half, at, 0:2 * HEAD] = twice
        kx[half, at, 2 * HEAD:4 * HEAD] = jnp.where(wanted == col, 1.0, 0.0).astype(jnp.bfloat16)


def attention(chunk_count, chunk_rows, total_rows, span_rows, kx, kt, vx, qx, qs, dox, dos, score, dkv, dq_ref, after_chunk, tile_order, after_tile):
    tiles = total_rows // KEY_TILE
    heads = dq_ref.shape[1] // HEAD

    def chunk_at(chunk):
        return pl.ds(chunk * chunk_rows, chunk_rows)

    def tile_at(tile):
        first_row = tile * KEY_TILE
        if not isinstance(tile, int):
            first_row = pl.multiple_of(first_row, KEY_TILE)
        return pl.ds(first_row, KEY_TILE)

    def score_tile(chunk, tile, top):
        half = chunk * 2 // chunk_count
        s = dot(kx[half, tile_at(tile), :], qx[chunk_at(chunk), :], NT)
        score[chunk % 2, tile_at(tile), :] = s
        return jnp.maximum(top, jnp.max(s.reshape(KEY_TILE // 8, 8, chunk_rows), axis=0))

    def exp_tile(chunk, tile, peak, total):
        e = jnp.exp2(score[chunk % 2, tile_at(tile), :] - peak)
        score[chunk % 2, tile_at(tile), :] = e
        return total + jnp.sum(e.reshape(KEY_TILE // 8, 8, chunk_rows), axis=0)

    top_start = jnp.full((8, chunk_rows), hidden, jnp.float32)
    zero = jnp.zeros((8, chunk_rows), jnp.float32)
    top = top_start
    for tile in range(tiles):
        top = score_tile(0, tile, top)
    for chunk in range(chunk_count):
        peak = jnp.max(top, axis=0, keepdims=True)

        top, total = top_start, zero
        for tile in range(tiles):
            if chunk + 1 < chunk_count:
                top = score_tile(chunk + 1, tile, top)
            total = exp_tile(chunk, tile, peak, total)
        inverse = 1.0 / jnp.sum(total, axis=0, keepdims=True)

        def second(tile, dqt, chunk=chunk, inverse=inverse):
            at = tile_at(tile)
            probs = score[chunk % 2, at, :] * inverse
            dprobs = dot(vx[at, :], dox[chunk_at(chunk), :], NT)
            dscores = (probs * dprobs).astype(jnp.bfloat16)
            add = dot(probs.astype(jnp.bfloat16), dos[chunk_at(chunk), :])
            add = add + dot(dscores, qs[chunk_at(chunk), :])
            if chunk == 0:
                dkv[at, :] = add
            else:
                dkv[at, :] += add
            return dqt + dot(kt[:, at], dscores)

        dqt = jnp.zeros((HEAD, chunk_rows), jnp.float32)
        for turn in range(tiles):
            if chunk + 1 < chunk_count:
                dqt = second(turn, dqt)
            else:
                dqt = second(tile_order(turn), dqt)
                after_tile(turn)
        dq = (dqt * softmax_scale).T
        half = chunk * 2 // chunk_count
        first_head = chunk * CHUNK_HEADS % heads
        for pair in range(CHUNK_HEADS // 2):
            parts = [
                dq[(2 * pair + side) * span_rows:(2 * pair + side + 1) * span_rows, :]
                for side in range(2)
            ]
            dq_ref[
                pl.ds(half * span_rows, span_rows),
                pl.ds((first_head + 2 * pair) * HEAD, 2 * HEAD),
            ] = jnp.concatenate(parts, axis=1).astype(jnp.bfloat16)
        after_chunk(chunk)


def weight_pieces(share, most):
    return next(count for count in (4, 2, 1) if count <= most and share % (16 * count) == 0)


def backward_kernel(
    ctx_size, tp_size,
    table_ref, q_ref, do_ref, fo_ref, kv_ref, w_ref,
    dq_ref, grad_ref, wall_ref,
    qx, qs, dox, dos, kx, kt, vx, score, dkv,
    gathered, mate_sum, row_out, row_in, far_out, far_in,
    gz_send, gz_recv, gy_send, gy_recv, gm_send, gm_recv,
    rm_send, rm_recv, ry_send, ry_recv, rz_send, rz_recv,
    wx_send, wx_recv, wm_send, wm_recv, own_sem, t_send, t_recv,
):
    tokens = q_ref.shape[0]
    total_rows = gathered.shape[0]
    far = ctx_size // 4
    me = lax.axis_index("ctx")
    tp = lax.axis_index("tp")
    hi, mid, core = me // 4, lax.rem(me // 2, 2), lax.rem(me, 2)

    def place(h, m, k):
        return h * 4 + m * 2 + k

    def around(step):
        return lax.rem(hi + step, far)

    def behind(step):
        return lax.rem(hi + far - step, far)

    def block(owner):
        return gathered.at[pl.ds(pl.multiple_of(owner * tokens, tokens), tokens), :]

    def send(src, dst, send_sem, recv_sem, axis, target):
        copy = pltpu.make_async_remote_copy(
            src_ref=src, dst_ref=dst, send_sem=send_sem, recv_sem=recv_sem,
            device_id={axis: target}, device_id_type=pl.DeviceIdType.MESH,
        )
        copy.start()
        return copy

    row_mate, core_mate = place(hi, 1 - mid, core), place(hi, mid, 1 - core)
    partners = [("ctx", place(around(step), mid, core)) for step in range(1, far)]
    partners += [("ctx", row_mate), ("ctx", core_mate)]
    partners += [("tp", lax.rem(tp + step, tp_size)) for step in range(1, tp_size)]
    barrier = pltpu.get_barrier_semaphore()
    for axis, target in partners:
        pl.semaphore_signal(barrier, inc=1, device_id={axis: target}, device_id_type=pl.DeviceIdType.MESH)
    pl.semaphore_wait(barrier, len(partners))

    waits = []
    for step in range(1, far):
        waits.append(send(kv_ref, block(me), gz_send.at[step], gz_recv.at[step], "ctx", place(around(step), mid, core)))
    from_far = list(waits)
    from_row = [send(kv_ref, block(me), gy_send.at[0], gy_recv.at[0], "ctx", row_mate)]
    from_core = [send(kv_ref, block(me), gm_send.at[0, 0], gm_recv.at[0, 0], "ctx", core_mate)]

    features = w_ref.shape[0] // tp_size
    share = features // 2
    pieces = weight_pieces(share, wx_send.shape[1])
    piece_rows = share // pieces
    own_copy = pltpu.make_async_copy(
        w_ref.at[pl.ds(pl.multiple_of(tp * features, 16), features), :], wall_ref.at[0], own_sem
    )
    own_copy.start()

    def wall_piece(step, side, piece):
        first = pl.multiple_of(side * share + piece * piece_rows, 16)
        return wall_ref.at[step, pl.ds(first, piece_rows), :]

    weight_in = {}
    for piece in range(pieces):
        for step in range(1, tp_size):
            target = lax.rem(tp + step, tp_size)
            first = pl.multiple_of(target * features + core * share + piece * piece_rows, 16)
            weight_in[step, piece] = send(
                w_ref.at[pl.ds(first, piece_rows), :], wall_piece(step, core, piece),
                wx_send.at[step, piece], wx_recv.at[step, piece], "tp", target,
            )
    weight_mate = []

    first_span = me * 2
    spread_queries(table_ref, first_span, 0, q_ref, do_ref, fo_ref, qx, qs, dox, dos)
    for step in range(1, far):
        from_far[step - 1].wait_recv()
        here = block(place(behind(step), mid, core))
        from_row.append(send(here, here, gy_send.at[step], gy_recv.at[step], "ctx", row_mate))
        from_core.append(send(here, here, gm_send.at[step, 0], gm_recv.at[step, 0], "ctx", core_mate))
    spread_queries(table_ref, first_span, 1, q_ref, do_ref, fo_ref, qx, qs, dox, dos)
    for step in range(far):
        from_row[step].wait_recv()
        here = block(place(behind(step), 1 - mid, core))
        from_core.append(send(here, here, gm_send.at[step, 1], gm_recv.at[step, 1], "ctx", core_mate))

    def take(owner, ref):
        first_row = pl.multiple_of(owner * tokens, tokens)
        spread_keys(table_ref, first_span, first_row, ref[...], kx, kt, vx)

    take(me, kv_ref)

    @pl.loop(1, 2 * far)
    def _(turn):
        owner = place(behind(turn // 2), lax.rem(mid + lax.rem(turn, 2), 2), core)
        take(owner, block(owner))

    for copy in from_core:
        copy.wait_recv()

    @pl.loop(0, 2 * far)
    def _(turn):
        owner = place(behind(turn // 2), lax.rem(mid + lax.rem(turn, 2), 2), 1 - core)
        take(owner, block(owner))

    for copy in from_far + from_row + from_core:
        copy.wait_send()

    def share_weights(piece):
        for step in range(1, tp_size):
            weight_in[step, piece].wait_recv()
            here = wall_piece(step, core, piece)
            weight_mate.append(
                send(here, here, wm_send.at[step, piece], wm_recv.at[step, piece], "ctx", core_mate)
            )

    def after_chunk(chunk):
        if 1 <= chunk <= pieces:
            share_weights(chunk - 1)

    def turn_place(turn):
        return around(turn % far + 1), (1 - mid if turn < far else mid)

    def tile_order(turn):
        h, m = turn_place(turn)
        return h * 2 + m

    def part(turn, k):
        h, m = turn_place(turn)
        return pl.ds(pl.multiple_of(place(h, m, k) * tokens, tokens), tokens)

    to_core, to_row, to_far = [], [], []

    def pass_on(turn):
        to_core[turn].wait_recv()
        total = dkv[part(turn, core), :] + mate_sum[turn]
        step = turn % far
        if turn < far:
            row_out[step] = total.astype(jnp.bfloat16)
            to_row.append(send(row_out.at[step], row_in.at[step], ry_send.at[step], ry_recv.at[step], "ctx", row_mate))
            return
        to_row[step].wait_recv()
        total = total + row_in[step].astype(jnp.float32)
        if step + 1 < far:
            far_out[step] = total.astype(jnp.bfloat16)
            h, _ = turn_place(turn)
            to_far.append(
                send(far_out.at[step], far_in.at[step], rz_send.at[step], rz_recv.at[step], "ctx", place(h, mid, core))
            )
            return
        for copy in to_far:
            copy.wait_recv()
        for step in range(far - 1):
            total = total + far_in[step].astype(jnp.float32)
        grad_ref[0] = total.astype(jnp.bfloat16)

    lag = 3

    def after_tile(turn):
        to_core.append(
            send(dkv.at[part(turn, 1 - core), :], mate_sum.at[turn], rm_send.at[turn], rm_recv.at[turn], "ctx", core_mate)
        )
        if turn >= lag:
            pass_on(turn - lag)

    chunk_rows = CHUNK_HEADS * tokens // 2
    chunk_count = qx.shape[0] // chunk_rows
    attention(
        chunk_count, chunk_rows, total_rows, tokens // 2, kx, kt, vx, qx, qs, dox, dos, score, dkv, dq_ref,
        after_chunk, tile_order, after_tile,
    )
    for turn in range(2 * far - lag, 2 * far):
        pass_on(turn)
    for piece in range(chunk_count - 1, pieces):
        share_weights(piece)
    last = []
    for step in range(1, tp_size):
        last.append(
            send(
                grad_ref.at[0], grad_ref.at[step],
                t_send.at[step], t_recv.at[step], "tp", lax.rem(tp + step, tp_size),
            )
        )
    for copy in to_core + to_row + to_far + list(weight_in.values()):
        copy.wait_send()
    for copy in weight_mate + last:
        copy.wait()
    own_copy.wait()


def feature_chunks(features):
    if features % 128:
        return [(0, features)]
    step = 1024
    return [(first, min(step, features - first)) for first in range(0, features, step)]


def project_kernel(chunks, grad_ref, w_ref, out_ref, w_buf, out_buf, in_sem, out_sem):
    tp_size = w_ref.shape[0]
    arrivals = []
    for index, (first, count) in enumerate(chunks):
        arrivals.append([
            pltpu.make_async_copy(
                w_ref.at[step, pl.ds(first, count), :],
                w_buf.at[pl.ds(first, count), pl.ds(step * 2 * HEAD, 2 * HEAD)],
                in_sem.at[index, step],
            )
            for step in range(tp_size)
        ])
        for copy in arrivals[-1]:
            copy.start()
    grad = jnp.concatenate([grad_ref[step] for step in range(tp_size)], axis=1)
    leaving = []
    for index, (first, count) in enumerate(chunks):
        for copy in arrivals[index]:
            copy.wait()
        out_buf[:, first:first + count] = dot(grad, w_buf[first:first + count, :], NT).astype(jnp.bfloat16)
        leaving.append(
            pltpu.make_async_copy(
                out_buf.at[:, pl.ds(first, count)], out_ref.at[:, pl.ds(first, count)], out_sem.at[index]
            )
        )
        leaving[-1].start()
    for copy in leaving:
        copy.wait()


def scratch(tokens, heads, ctx_size, tp_size):
    total_rows = tokens * ctx_size
    rows = tokens * heads
    chunk_rows = CHUNK_HEADS * tokens // 2
    far = ctx_size // 4
    block = (tokens, 2 * HEAD)
    sems = pltpu.SemaphoreType.DMA
    return [
        pltpu.VMEM((rows, 4 * HEAD), jnp.bfloat16),
        pltpu.VMEM((rows, 2 * HEAD), jnp.bfloat16),
        pltpu.VMEM((rows, 2 * HEAD), jnp.bfloat16),
        pltpu.VMEM((rows, 2 * HEAD), jnp.bfloat16),
        pltpu.VMEM((2, total_rows, 4 * HEAD), jnp.bfloat16),
        pltpu.VMEM((HEAD, total_rows), jnp.bfloat16),
        pltpu.VMEM((total_rows, 2 * HEAD), jnp.bfloat16),
        pltpu.VMEM((2, total_rows, chunk_rows), jnp.float32),
        pltpu.VMEM((total_rows, 2 * HEAD), jnp.float32),
        pltpu.VMEM((total_rows, 2 * HEAD), jnp.bfloat16),
        pltpu.VMEM((2 * far,) + block, jnp.float32),
        pltpu.VMEM((far,) + block, jnp.bfloat16),
        pltpu.VMEM((far,) + block, jnp.bfloat16),
        pltpu.VMEM((far,) + block, jnp.bfloat16),
        pltpu.VMEM((far,) + block, jnp.bfloat16),
        sems((far,)), sems((far,)), sems((far,)), sems((far,)), sems((far, 2)), sems((far, 2)),
        sems((2 * far,)), sems((2 * far,)), sems((far,)), sems((far,)), sems((far,)), sems((far,)),
        sems((tp_size, 4)), sems((tp_size, 4)), sems((tp_size, 4)), sems((tp_size, 4)), sems(()),
        sems((tp_size,)), sems((tp_size,)),
    ]


def on_device(queries, keys_values, forward_out, out_grad, kv_weight, span_table):
    tokens = queries.shape[0]
    heads = queries.shape[1] // HEAD
    tp_size = lax.axis_size("tp")
    ctx_size = lax.axis_size("ctx")
    features = kv_weight.shape[0] // tp_size
    vmem = pl.BlockSpec(memory_space=pltpu.VMEM)
    anywhere = pl.BlockSpec(memory_space=pl.ANY)
    query_grad, kv_grad, weights = pl.pallas_call(
        functools.partial(backward_kernel, ctx_size, tp_size),
        out_shape=(
            jax.ShapeDtypeStruct(queries.shape, jnp.bfloat16),
            jax.ShapeDtypeStruct((tp_size, tokens, 2 * HEAD), jnp.bfloat16),
            jax.ShapeDtypeStruct((tp_size, features, 2 * HEAD), jnp.bfloat16),
        ),
        in_specs=[pl.BlockSpec(memory_space=pltpu.SMEM)] + [vmem] * 4 + [anywhere],
        out_specs=(vmem, vmem, anywhere),
        scratch_shapes=scratch(tokens, heads, ctx_size, tp_size),
        compiler_params=pltpu.CompilerParams(
            vmem_limit_bytes=56 * 2**20, collective_id=0, has_side_effects=True
        ),
    )(span_table, queries, out_grad, forward_out, keys_values, kv_weight)
    chunks = feature_chunks(features)
    input_grad = pl.pallas_call(
        functools.partial(project_kernel, chunks),
        out_shape=jax.ShapeDtypeStruct((tokens, features), jnp.bfloat16),
        in_specs=[vmem, anywhere],
        out_specs=anywhere,
        scratch_shapes=[
            pltpu.VMEM((features, tp_size * 2 * HEAD), jnp.bfloat16),
            pltpu.VMEM((tokens, features), jnp.bfloat16),
            pltpu.SemaphoreType.DMA((len(chunks), tp_size)),
            pltpu.SemaphoreType.DMA((len(chunks),)),
        ],
        compiler_params=pltpu.CompilerParams(vmem_limit_bytes=24 * 2**20),
    )(kv_grad, weights)
    return (query_grad, input_grad)


def solution(mesh):
    placed = (P("ctx", "tp"), P("ctx", "tp"), P("ctx", "tp"), P("ctx", "tp"), P(None, "tp"), P())
    return jax.shard_map(
        on_device,
        mesh=mesh,
        in_specs=placed,
        out_specs=(P("ctx", "tp"), P("ctx", "tp")),
        check_vma=False,
    )
```

```python
import functools

import jax
import jax.numpy as jnp
from jax import lax
from jax.experimental import pallas as pl
from jax.experimental.pallas import tpu as pltpu
from jax.sharding import PartitionSpec as P

HEAD = 64
CHUNK_HEADS = 8
KEY_TILE = 256
softmax_scale = 0.125
log2_e = 1.4426950408889634
hidden = -1e30

NT = (((1,), (1,)), ((), ()))
NN = (((1,), (0,)), ((), ()))


def dot(a, b, dims=NN):
    return lax.dot_general(a, b, dims, preferred_element_type=jnp.float32)


def spread_queries(table_ref, first_span, half, q_ref, do_ref, fo_ref, qx, qs, dox, dos):
    span_rows = q_ref.shape[0] // 2
    heads = q_ref.shape[1] // HEAD
    span = table_ref[first_span + half]
    row = lax.broadcasted_iota(jnp.int32, (span_rows, 2 * HEAD), 0)
    col = lax.broadcasted_iota(jnp.int32, (span_rows, 2 * HEAD), 1)
    blocked = jnp.where(col < HEAD, col - row, col - HEAD - span) > 0
    mask_cols = jnp.where(blocked, hidden, 0.0).astype(jnp.bfloat16)
    lane = lax.broadcasted_iota(jnp.int32, (span_rows, HEAD), 1)
    rows = pl.ds(half * span_rows, span_rows)
    for head in range(heads):
        pair = pl.ds(head // 2 * 2 * HEAD, 2 * HEAD)
        low = head % 2 * HEAD
        at = pl.ds((half * heads + head) * span_rows, span_rows)
        query = q_ref[rows, pair].astype(jnp.float32)[:, low:low + HEAD]
        grad = do_ref[rows, pair].astype(jnp.float32)[:, low:low + HEAD]
        forward = fo_ref[rows, pair].astype(jnp.float32)[:, low:low + HEAD]
        scaled = query * (softmax_scale * log2_e)
        top = scaled.astype(jnp.bfloat16).astype(jnp.float32)
        qx[at, 0:2 * HEAD] = jnp.concatenate([top, scaled - top], axis=1).astype(jnp.bfloat16)
        qx[at, 2 * HEAD:4 * HEAD] = mask_cols
        blank = jnp.zeros((span_rows, HEAD), jnp.float32)
        qs[at, :] = jnp.concatenate([query * softmax_scale, blank], axis=1).astype(jnp.bfloat16)
        dos[at, :] = jnp.concatenate([blank, grad], axis=1).astype(jnp.bfloat16)
        left = -jnp.sum(grad * forward, axis=1, keepdims=True)
        tail = jnp.zeros((span_rows, HEAD), jnp.float32)
        for place in range(3):
            part = left.astype(jnp.bfloat16).astype(jnp.float32)
            tail = jnp.where(lane == place, part, tail)
            left = left - part
        dox[at, :] = jnp.concatenate([grad, tail], axis=1).astype(jnp.bfloat16)


def spread_keys(table_ref, first_span, first_row, block, kx, kt, vx):
    rows = block.shape[0]
    span_rows = rows // 2
    wide = block.astype(jnp.float32)
    key, value = wide[:, :HEAD], wide[:, HEAD:]
    lane = lax.broadcasted_iota(jnp.int32, (rows, HEAD), 1)
    ones = jnp.where(lane < 3, 1.0, 0.0)
    at = pl.ds(first_row, rows)
    vx[at, :] = jnp.concatenate([value, ones], axis=1).astype(jnp.bfloat16)
    eye = (
        lax.broadcasted_iota(jnp.int32, (HEAD, HEAD), 0)
        == lax.broadcasted_iota(jnp.int32, (HEAD, HEAD), 1)
    ).astype(jnp.bfloat16)
    kt[:, at] = dot(eye, key.astype(jnp.bfloat16), NT).astype(jnp.bfloat16)
    twice = jnp.concatenate([key, key], axis=1).astype(jnp.bfloat16)
    row = lax.broadcasted_iota(jnp.int32, (rows, 2 * HEAD), 0)
    col = lax.broadcasted_iota(jnp.int32, (rows, 2 * HEAD), 1)
    span_index = first_row // span_rows
    span = jnp.where(row < span_rows, table_ref[span_index], table_ref[span_index + 1])
    inner = jnp.where(row < span_rows, row, row - span_rows)
    for half in range(2):
        own = table_ref[first_span + half]
        wanted = jnp.where(col < HEAD, jnp.where(span == own, inner, -1), span + HEAD)
        kx[half, at, 0:2 * HEAD] = twice
        kx[half, at, 2 * HEAD:4 * HEAD] = jnp.where(wanted == col, 1.0, 0.0).astype(jnp.bfloat16)


def attention(chunk_count, chunk_rows, total_rows, span_rows, kx, kt, vx, qx, qs, dox, dos, score, dkv, dq_ref, after_chunk, tile_order, after_tile):
    tiles = total_rows // KEY_TILE
    heads = dq_ref.shape[1] // HEAD

    def chunk_at(chunk):
        return pl.ds(chunk * chunk_rows, chunk_rows)

    def tile_at(tile):
        first_row = tile * KEY_TILE
        if not isinstance(tile, int):
            first_row = pl.multiple_of(first_row, KEY_TILE)
        return pl.ds(first_row, KEY_TILE)

    def score_tile(chunk, tile, top):
        half = chunk * 2 // chunk_count
        s = dot(kx[half, tile_at(tile), :], qx[chunk_at(chunk), :], NT)
        score[chunk % 2, tile_at(tile), :] = s
        return jnp.maximum(top, jnp.max(s.reshape(KEY_TILE // 8, 8, chunk_rows), axis=0))

    def exp_tile(chunk, tile, peak, total):
        e = jnp.exp2(score[chunk % 2, tile_at(tile), :] - peak)
        score[chunk % 2, tile_at(tile), :] = e
        return total + jnp.sum(e.reshape(KEY_TILE // 8, 8, chunk_rows), axis=0)

    top_start = jnp.full((8, chunk_rows), hidden, jnp.float32)
    zero = jnp.zeros((8, chunk_rows), jnp.float32)
    top = top_start
    for tile in range(tiles):
        top = score_tile(0, tile, top)
    for chunk in range(chunk_count):
        peak = jnp.max(top, axis=0, keepdims=True)

        top, total = top_start, zero
        for tile in range(tiles):
            if chunk + 1 < chunk_count:
                top = score_tile(chunk + 1, tile, top)
            total = exp_tile(chunk, tile, peak, total)
        inverse = 1.0 / jnp.sum(total, axis=0, keepdims=True)

        def second(tile, dqt, chunk=chunk, inverse=inverse):
            at = tile_at(tile)
            probs = score[chunk % 2, at, :] * inverse
            dprobs = dot(vx[at, :], dox[chunk_at(chunk), :], NT)
            dscores = (probs * dprobs).astype(jnp.bfloat16)
            add = dot(probs.astype(jnp.bfloat16), dos[chunk_at(chunk), :])
            add = add + dot(dscores, qs[chunk_at(chunk), :])
            if chunk == 0:
                dkv[at, :] = add
            else:
                dkv[at, :] += add
            return dqt + dot(kt[:, at], dscores)

        dqt = jnp.zeros((HEAD, chunk_rows), jnp.float32)
        for turn in range(tiles):
            if chunk + 1 < chunk_count:
                dqt = second(turn, dqt)
            else:
                dqt = second(tile_order(turn), dqt)
                after_tile(turn)
        dq = (dqt * softmax_scale).T
        half = chunk * 2 // chunk_count
        first_head = chunk * CHUNK_HEADS % heads
        for pair in range(CHUNK_HEADS // 2):
            parts = [
                dq[(2 * pair + side) * span_rows:(2 * pair + side + 1) * span_rows, :]
                for side in range(2)
            ]
            dq_ref[
                pl.ds(half * span_rows, span_rows),
                pl.ds((first_head + 2 * pair) * HEAD, 2 * HEAD),
            ] = jnp.concatenate(parts, axis=1).astype(jnp.bfloat16)
        after_chunk(chunk)


def weight_pieces(share, most):
    return next(count for count in (4, 2, 1) if count <= most and share % (16 * count) == 0)


def backward_kernel(
    ctx_size, tp_size,
    table_ref, q_ref, do_ref, fo_ref, kv_ref, w_ref,
    dq_ref, out_ref,
    qx, qs, dox, dos, kx, kt, vx, score, dkv,
    gathered, mate_sum, row_out, row_in, far_out, far_in, grad_ref, wall_ref, staged, out_buf,
    gz_send, gz_recv, gy_send, gy_recv, gm_send, gm_recv,
    rm_send, rm_recv, ry_send, ry_recv, rz_send, rz_recv,
    wx_send, wx_recv, wm_send, wm_recv, own_sem, t_send, t_recv,
    stage_sem, bx_send, bx_recv, bz_send, bz_recv, by_send, by_recv, bm_send, bm_recv, out_sem,
):
    tokens = q_ref.shape[0]
    total_rows = gathered.shape[0]
    far = ctx_size // 4
    me = lax.axis_index("ctx")
    tp = lax.axis_index("tp")
    hi, mid, core = me // 4, lax.rem(me // 2, 2), lax.rem(me, 2)

    def place(h, m, k):
        return h * 4 + m * 2 + k

    def around(step):
        return lax.rem(hi + step, far)

    def behind(step):
        return lax.rem(hi + far - step, far)

    def block(owner):
        return gathered.at[pl.ds(pl.multiple_of(owner * tokens, tokens), tokens), :]

    def send(src, dst, send_sem, recv_sem, axis, target):
        copy = pltpu.make_async_remote_copy(
            src_ref=src, dst_ref=dst, send_sem=send_sem, recv_sem=recv_sem,
            device_id={axis: target}, device_id_type=pl.DeviceIdType.MESH,
        )
        copy.start()
        return copy

    row_mate, core_mate = place(hi, 1 - mid, core), place(hi, mid, 1 - core)
    partners = [("ctx", place(around(step), mid, core)) for step in range(1, far)]
    partners += [("ctx", row_mate), ("ctx", core_mate)]
    partners += [("tp", lax.rem(tp + step, tp_size)) for step in range(1, tp_size)]
    features = w_ref.shape[0] // tp_size
    spread = spread_block(features, ctx_size)
    spread_rows = spread * ctx_size
    share = (features - spread_rows) // 2
    pieces = weight_pieces(share, wx_send.shape[1])
    piece_rows = share // pieces
    own_copy = pltpu.make_async_copy(
        w_ref.at[pl.ds(pl.multiple_of(tp * features, 16), features), :], wall_ref.at[0], own_sem
    )
    staging = []
    for step in range(1, tp_size):
        target = lax.rem(tp + step, tp_size) * features
        first = pl.multiple_of(target + me * spread, 16)
        staging.append(pltpu.make_async_copy(
            w_ref.at[pl.ds(first, spread), :], staged.at[step - 1, pl.ds(0, spread), :], stage_sem.at[step, 0]
        ))
        first = pl.multiple_of(target + spread_rows + core * share, 16)
        staging.append(pltpu.make_async_copy(
            w_ref.at[pl.ds(first, share), :], staged.at[step - 1, pl.ds(spread, share), :], stage_sem.at[step, 1]
        ))
    for copy in staging:
        copy.start()

    barrier = pltpu.get_barrier_semaphore()
    for axis, target in partners:
        pl.semaphore_signal(barrier, inc=1, device_id={axis: target}, device_id_type=pl.DeviceIdType.MESH)
    pl.semaphore_wait(barrier, len(partners))

    waits = []
    for step in range(1, far):
        waits.append(send(kv_ref, block(me), gz_send.at[step], gz_recv.at[step], "ctx", place(around(step), mid, core)))
    from_far = list(waits)
    from_row = [send(kv_ref, block(me), gy_send.at[0], gy_recv.at[0], "ctx", row_mate)]
    from_core = [send(kv_ref, block(me), gm_send.at[0, 0], gm_recv.at[0, 0], "ctx", core_mate)]

    own_copy.start()
    for copy in staging:
        copy.wait()

    def wall_piece(step, side, piece):
        first = pl.multiple_of(spread_rows + side * share + piece * piece_rows, 16)
        return wall_ref.at[step, pl.ds(first, piece_rows), :]

    def wall_block(step, owner):
        return wall_ref.at[step, pl.ds(pl.multiple_of(owner * spread, 16), spread), :]

    block_in = {}
    for step in range(1, tp_size):
        block_in[step] = send(
            staged.at[step - 1, pl.ds(0, spread), :], wall_block(step, me),
            bx_send.at[step], bx_recv.at[step], "tp", lax.rem(tp + step, tp_size),
        )
    weight_in = {}
    for piece in range(pieces):
        for step in range(1, tp_size):
            weight_in[step, piece] = send(
                staged.at[step - 1, pl.ds(spread + piece * piece_rows, piece_rows), :], wall_piece(step, core, piece),
                wx_send.at[step, piece], wx_recv.at[step, piece], "tp", lax.rem(tp + step, tp_size),
            )
    weight_mate, block_far, block_row, block_core = [], {}, {}, []

    def block_to_mates(step, hop):
        here = wall_block(step, place(behind(hop), mid, core))
        block_row[step, hop] = send(here, here, by_send.at[step, hop], by_recv.at[step, hop], "ctx", row_mate)
        block_core.append(send(here, here, bm_send.at[step, hop, 0], bm_recv.at[step, hop, 0], "ctx", core_mate))

    def spread_own_blocks():
        for step in range(1, tp_size):
            block_in[step].wait_recv()
            here = wall_block(step, me)
            for hop in range(1, far):
                block_far[step, hop] = send(
                    here, here, bz_send.at[step, hop], bz_recv.at[step, hop], "ctx", place(around(hop), mid, core)
                )
            block_to_mates(step, 0)

    def spread_far_blocks():
        for step in range(1, tp_size):
            for hop in range(1, far):
                block_far[step, hop].wait_recv()
                block_to_mates(step, hop)

    def spread_row_blocks():
        for step in range(1, tp_size):
            for hop in range(far):
                block_row[step, hop].wait_recv()
                here = wall_block(step, place(behind(hop), 1 - mid, core))
                block_core.append(
                    send(here, here, bm_send.at[step, hop, 1], bm_recv.at[step, hop, 1], "ctx", core_mate)
                )

    first_span = me * 2
    spread_queries(table_ref, first_span, 0, q_ref, do_ref, fo_ref, qx, qs, dox, dos)
    for step in range(1, far):
        from_far[step - 1].wait_recv()
        here = block(place(behind(step), mid, core))
        from_row.append(send(here, here, gy_send.at[step], gy_recv.at[step], "ctx", row_mate))
        from_core.append(send(here, here, gm_send.at[step, 0], gm_recv.at[step, 0], "ctx", core_mate))
    spread_queries(table_ref, first_span, 1, q_ref, do_ref, fo_ref, qx, qs, dox, dos)
    for step in range(far):
        from_row[step].wait_recv()
        here = block(place(behind(step), 1 - mid, core))
        from_core.append(send(here, here, gm_send.at[step, 1], gm_recv.at[step, 1], "ctx", core_mate))

    def take(owner, ref):
        first_row = pl.multiple_of(owner * tokens, tokens)
        spread_keys(table_ref, first_span, first_row, ref[...], kx, kt, vx)

    take(me, kv_ref)

    @pl.loop(1, 2 * far)
    def _(turn):
        owner = place(behind(turn // 2), lax.rem(mid + lax.rem(turn, 2), 2), core)
        take(owner, block(owner))

    for copy in from_core:
        copy.wait_recv()

    @pl.loop(0, 2 * far)
    def _(turn):
        owner = place(behind(turn // 2), lax.rem(mid + lax.rem(turn, 2), 2), 1 - core)
        take(owner, block(owner))

    for copy in from_far + from_row + from_core:
        copy.wait_send()

    def share_weights(piece):
        for step in range(1, tp_size):
            weight_in[step, piece].wait_recv()
            here = wall_piece(step, core, piece)
            weight_mate.append(
                send(here, here, wm_send.at[step, piece], wm_recv.at[step, piece], "ctx", core_mate)
            )

    spread_own_blocks()

    def after_chunk(chunk):
        if chunk == 0:
            spread_far_blocks()
        if chunk == 1:
            spread_row_blocks()
        if chunk + 1 < chunk_count and chunk < pieces:
            share_weights(chunk)

    def turn_place(turn):
        return around(turn % far + 1), (1 - mid if turn < far else mid)

    def tile_order(turn):
        h, m = turn_place(turn)
        return h * 2 + m

    def part(turn, k):
        h, m = turn_place(turn)
        return pl.ds(pl.multiple_of(place(h, m, k) * tokens, tokens), tokens)

    to_core, to_row, to_far = [], [], []

    def pass_on(turn):
        to_core[turn].wait_recv()
        total = dkv[part(turn, core), :] + mate_sum[turn]
        step = turn % far
        if turn < far:
            row_out[step] = total.astype(jnp.bfloat16)
            to_row.append(send(row_out.at[step], row_in.at[step], ry_send.at[step], ry_recv.at[step], "ctx", row_mate))
            return
        to_row[step].wait_recv()
        total = total + row_in[step].astype(jnp.float32)
        if step + 1 < far:
            far_out[step] = total.astype(jnp.bfloat16)
            h, _ = turn_place(turn)
            to_far.append(
                send(far_out.at[step], far_in.at[step], rz_send.at[step], rz_recv.at[step], "ctx", place(h, mid, core))
            )
            return
        for copy in to_far:
            copy.wait_recv()
        for step in range(far - 1):
            total = total + far_in[step].astype(jnp.float32)
        grad_ref[0] = total.astype(jnp.bfloat16)

    lag = 3

    def after_tile(turn):
        to_core.append(
            send(dkv.at[part(turn, 1 - core), :], mate_sum.at[turn], rm_send.at[turn], rm_recv.at[turn], "ctx", core_mate)
        )
        if turn >= lag:
            pass_on(turn - lag)

    chunk_rows = CHUNK_HEADS * tokens // 2
    chunk_count = qx.shape[0] // chunk_rows
    attention(
        chunk_count, chunk_rows, total_rows, tokens // 2, kx, kt, vx, qx, qs, dox, dos, score, dkv, dq_ref,
        after_chunk, tile_order, after_tile,
    )
    for turn in range(2 * far - lag, 2 * far):
        if turn + 1 == 2 * far:
            for piece in range(chunk_count - 1, pieces):
                share_weights(piece)
        pass_on(turn)
    last = []
    for step in range(1, tp_size):
        last.append(
            send(
                grad_ref.at[0], grad_ref.at[step],
                t_send.at[step], t_recv.at[step], "tp", lax.rem(tp + step, tp_size),
            )
        )
    for copy in last + weight_mate + block_core:
        copy.wait_recv()
    own_copy.wait()
    grad = jnp.concatenate([grad_ref[step] for step in range(tp_size)], axis=1)
    leaving = []
    for index, (first, count) in enumerate(feature_chunks(features)):
        at = pl.ds(first, count)
        weights = jnp.concatenate([wall_ref[step, at, :] for step in range(tp_size)], axis=1)
        out_buf[:, at] = dot(grad, weights, NT).astype(jnp.bfloat16)
        leaving.append(pltpu.make_async_copy(out_buf.at[:, at], out_ref.at[:, at], out_sem.at[index]))
        leaving[-1].start()
    for copy in to_core + to_row + to_far + last + weight_mate + block_core:
        copy.wait_send()
    for copies in (weight_in, block_in, block_far, block_row):
        for copy in copies.values():
            copy.wait_send()
    for copy in leaving:
        copy.wait()


def spread_block(features, ctx_size):
    return 16 * (features * 11 // (20 * 16 * ctx_size))


def feature_chunks(features):
    if features % 128:
        return [(0, features)]
    step = 1024
    return [(first, min(step, features - first)) for first in range(0, features, step)]


def scratch(tokens, heads, features, ctx_size, tp_size):
    total_rows = tokens * ctx_size
    rows = tokens * heads
    chunk_rows = CHUNK_HEADS * tokens // 2
    far = ctx_size // 4
    block = (tokens, 2 * HEAD)
    spread = spread_block(features, ctx_size)
    share = (features - spread * ctx_size) // 2
    sems = pltpu.SemaphoreType.DMA
    return [
        pltpu.VMEM((rows, 4 * HEAD), jnp.bfloat16),
        pltpu.VMEM((rows, 2 * HEAD), jnp.bfloat16),
        pltpu.VMEM((rows, 2 * HEAD), jnp.bfloat16),
        pltpu.VMEM((rows, 2 * HEAD), jnp.bfloat16),
        pltpu.VMEM((2, total_rows, 4 * HEAD), jnp.bfloat16),
        pltpu.VMEM((HEAD, total_rows), jnp.bfloat16),
        pltpu.VMEM((total_rows, 2 * HEAD), jnp.bfloat16),
        pltpu.VMEM((2, total_rows, chunk_rows), jnp.float32),
        pltpu.VMEM((total_rows, 2 * HEAD), jnp.float32),
        pltpu.VMEM((total_rows, 2 * HEAD), jnp.bfloat16),
        pltpu.VMEM((2 * far,) + block, jnp.float32),
        pltpu.VMEM((far,) + block, jnp.bfloat16),
        pltpu.VMEM((far,) + block, jnp.bfloat16),
        pltpu.VMEM((far,) + block, jnp.bfloat16),
        pltpu.VMEM((far,) + block, jnp.bfloat16),
        pltpu.VMEM((tp_size,) + block, jnp.bfloat16),
        pltpu.VMEM((tp_size, features, 2 * HEAD), jnp.bfloat16),
        pltpu.VMEM((tp_size - 1, spread + share, 2 * HEAD), jnp.bfloat16),
        pltpu.VMEM((tokens, features), jnp.bfloat16),
        sems((far,)), sems((far,)), sems((far,)), sems((far,)), sems((far, 2)), sems((far, 2)),
        sems((2 * far,)), sems((2 * far,)), sems((far,)), sems((far,)), sems((far,)), sems((far,)),
        sems((tp_size, 4)), sems((tp_size, 4)), sems((tp_size, 4)), sems((tp_size, 4)), sems(()),
        sems((tp_size,)), sems((tp_size,)),
        sems((tp_size, 2)), sems((tp_size,)), sems((tp_size,)), sems((tp_size, far)), sems((tp_size, far)),
        sems((tp_size, far)), sems((tp_size, far)), sems((tp_size, far, 2)), sems((tp_size, far, 2)),
        sems((len(feature_chunks(features)),)),
    ]


def on_device(queries, keys_values, forward_out, out_grad, kv_weight, span_table):
    tokens = queries.shape[0]
    heads = queries.shape[1] // HEAD
    tp_size = lax.axis_size("tp")
    ctx_size = lax.axis_size("ctx")
    features = kv_weight.shape[0] // tp_size
    vmem = pl.BlockSpec(memory_space=pltpu.VMEM)
    anywhere = pl.BlockSpec(memory_space=pl.ANY)
    return pl.pallas_call(
        functools.partial(backward_kernel, ctx_size, tp_size),
        out_shape=(
            jax.ShapeDtypeStruct(queries.shape, jnp.bfloat16),
            jax.ShapeDtypeStruct((tokens, features), jnp.bfloat16),
        ),
        in_specs=[pl.BlockSpec(memory_space=pltpu.SMEM)] + [vmem] * 4 + [anywhere],
        out_specs=(vmem, anywhere),
        scratch_shapes=scratch(tokens, heads, features, ctx_size, tp_size),
        compiler_params=pltpu.CompilerParams(
            vmem_limit_bytes=56 * 2**20, collective_id=0, has_side_effects=True
        ),
    )(span_table, queries, out_grad, forward_out, keys_values, kv_weight)


def solution(mesh):
    placed = (P("ctx", "tp"), P("ctx", "tp"), P("ctx", "tp"), P("ctx", "tp"), P(None, "tp"), P())
    return jax.shard_map(
        on_device,
        mesh=mesh,
        in_specs=placed,
        out_specs=(P("ctx", "tp"), P("ctx", "tp")),
        check_vma=False,
    )
```

```python
import functools

import jax
import jax.numpy as jnp
from jax import lax
from jax.experimental import pallas as pl
from jax.experimental.pallas import tpu as pltpu
from jax.sharding import PartitionSpec as P

HEAD = 64
CHUNK_HEADS = 8
KEY_TILE = 256
softmax_scale = 0.125
log2_e = 1.4426950408889634
hidden = -1e30

NT = (((1,), (1,)), ((), ()))
NN = (((1,), (0,)), ((), ()))


def dot(a, b, dims=NN):
    return lax.dot_general(a, b, dims, preferred_element_type=jnp.float32)


def spread_queries(table_ref, first_span, half, q_ref, do_ref, fo_ref, qx, qs, dox, dos):
    span_rows = q_ref.shape[0] // 2
    heads = q_ref.shape[1] // HEAD
    span = table_ref[first_span + half]
    row = lax.broadcasted_iota(jnp.int32, (span_rows, 2 * HEAD), 0)
    col = lax.broadcasted_iota(jnp.int32, (span_rows, 2 * HEAD), 1)
    blocked = jnp.where(col < HEAD, col - row, col - HEAD - span) > 0
    mask_cols = jnp.where(blocked, hidden, 0.0).astype(jnp.bfloat16)
    lane = lax.broadcasted_iota(jnp.int32, (span_rows, HEAD), 1)
    rows = pl.ds(half * span_rows, span_rows)
    for head in range(heads):
        pair = pl.ds(head // 2 * 2 * HEAD, 2 * HEAD)
        low = head % 2 * HEAD
        at = pl.ds((half * heads + head) * span_rows, span_rows)
        query = q_ref[rows, pair].astype(jnp.float32)[:, low:low + HEAD]
        grad = do_ref[rows, pair].astype(jnp.float32)[:, low:low + HEAD]
        forward = fo_ref[rows, pair].astype(jnp.float32)[:, low:low + HEAD]
        scaled = query * (softmax_scale * log2_e)
        top = scaled.astype(jnp.bfloat16).astype(jnp.float32)
        qx[at, 0:2 * HEAD] = jnp.concatenate([top, scaled - top], axis=1).astype(jnp.bfloat16)
        qx[at, 2 * HEAD:4 * HEAD] = mask_cols
        blank = jnp.zeros((span_rows, HEAD), jnp.float32)
        qs[at, :] = jnp.concatenate([query * softmax_scale, blank], axis=1).astype(jnp.bfloat16)
        dos[at, :] = jnp.concatenate([blank, grad], axis=1).astype(jnp.bfloat16)
        left = -jnp.sum(grad * forward, axis=1, keepdims=True)
        tail = jnp.zeros((span_rows, HEAD), jnp.float32)
        for place in range(3):
            part = left.astype(jnp.bfloat16).astype(jnp.float32)
            tail = jnp.where(lane == place, part, tail)
            left = left - part
        dox[at, :] = jnp.concatenate([grad, tail], axis=1).astype(jnp.bfloat16)


def spread_keys(table_ref, first_span, first_row, block, kx, kt, vx):
    rows = block.shape[0]
    span_rows = rows // 2
    wide = block.astype(jnp.float32)
    key, value = wide[:, :HEAD], wide[:, HEAD:]
    lane = lax.broadcasted_iota(jnp.int32, (rows, HEAD), 1)
    ones = jnp.where(lane < 3, 1.0, 0.0)
    at = pl.ds(first_row, rows)
    vx[at, :] = jnp.concatenate([value, ones], axis=1).astype(jnp.bfloat16)
    eye = (
        lax.broadcasted_iota(jnp.int32, (HEAD, HEAD), 0)
        == lax.broadcasted_iota(jnp.int32, (HEAD, HEAD), 1)
    ).astype(jnp.bfloat16)
    kt[:, at] = dot(eye, key.astype(jnp.bfloat16), NT).astype(jnp.bfloat16)
    twice = jnp.concatenate([key, key], axis=1).astype(jnp.bfloat16)
    row = lax.broadcasted_iota(jnp.int32, (rows, 2 * HEAD), 0)
    col = lax.broadcasted_iota(jnp.int32, (rows, 2 * HEAD), 1)
    span_index = first_row // span_rows
    span = jnp.where(row < span_rows, table_ref[span_index], table_ref[span_index + 1])
    inner = jnp.where(row < span_rows, row, row - span_rows)
    for half in range(2):
        own = table_ref[first_span + half]
        wanted = jnp.where(col < HEAD, jnp.where(span == own, inner, -1), span + HEAD)
        kx[half, at, 0:2 * HEAD] = twice
        kx[half, at, 2 * HEAD:4 * HEAD] = jnp.where(wanted == col, 1.0, 0.0).astype(jnp.bfloat16)


def attention(chunk_count, chunk_rows, total_rows, span_rows, kx, kt, vx, qx, qs, dox, dos, score, dkv, dq_ref, mid_chunk, after_chunk, tile_order, after_tile):
    tiles = total_rows // KEY_TILE
    heads = dq_ref.shape[1] // HEAD

    def chunk_at(chunk):
        return pl.ds(chunk * chunk_rows, chunk_rows)

    def tile_at(tile):
        first_row = tile * KEY_TILE
        if not isinstance(tile, int):
            first_row = pl.multiple_of(first_row, KEY_TILE)
        return pl.ds(first_row, KEY_TILE)

    def score_tile(chunk, tile, top):
        half = chunk * 2 // chunk_count
        s = dot(kx[half, tile_at(tile), :], qx[chunk_at(chunk), :], NT)
        score[chunk % 2, tile_at(tile), :] = s
        return jnp.maximum(top, jnp.max(s.reshape(KEY_TILE // 8, 8, chunk_rows), axis=0))

    def exp_tile(chunk, tile, peak, total):
        e = jnp.exp2(score[chunk % 2, tile_at(tile), :] - peak)
        score[chunk % 2, tile_at(tile), :] = e
        return total + jnp.sum(e.reshape(KEY_TILE // 8, 8, chunk_rows), axis=0)

    top_start = jnp.full((8, chunk_rows), hidden, jnp.float32)
    zero = jnp.zeros((8, chunk_rows), jnp.float32)
    top = top_start
    for tile in range(tiles):
        top = score_tile(0, tile, top)
    for chunk in range(chunk_count):
        peak = jnp.max(top, axis=0, keepdims=True)

        top, total = top_start, zero
        for tile in range(tiles):
            if chunk + 1 < chunk_count:
                top = score_tile(chunk + 1, tile, top)
            total = exp_tile(chunk, tile, peak, total)
        inverse = 1.0 / jnp.sum(total, axis=0, keepdims=True)
        mid_chunk(chunk)

        def second(tile, dqt, chunk=chunk, inverse=inverse):
            at = tile_at(tile)
            probs = score[chunk % 2, at, :] * inverse
            dprobs = dot(vx[at, :], dox[chunk_at(chunk), :], NT)
            dscores = (probs * dprobs).astype(jnp.bfloat16)
            add = dot(probs.astype(jnp.bfloat16), dos[chunk_at(chunk), :])
            add = add + dot(dscores, qs[chunk_at(chunk), :])
            if chunk == 0:
                dkv[at, :] = add
            else:
                dkv[at, :] += add
            return dqt + dot(kt[:, at], dscores)

        dqt = jnp.zeros((HEAD, chunk_rows), jnp.float32)
        for turn in range(tiles):
            if chunk + 1 < chunk_count:
                dqt = second(turn, dqt)
            else:
                dqt = second(tile_order(turn), dqt)
                after_tile(turn)
        dq = (dqt * softmax_scale).T
        half = chunk * 2 // chunk_count
        first_head = chunk * CHUNK_HEADS % heads
        for pair in range(CHUNK_HEADS // 2):
            parts = [
                dq[(2 * pair + side) * span_rows:(2 * pair + side + 1) * span_rows, :]
                for side in range(2)
            ]
            dq_ref[
                pl.ds(half * span_rows, span_rows),
                pl.ds((first_head + 2 * pair) * HEAD, 2 * HEAD),
            ] = jnp.concatenate(parts, axis=1).astype(jnp.bfloat16)
        after_chunk(chunk)


def weight_pieces(share, most):
    return next(count for count in (4, 2, 1) if count <= most and share % (16 * count) == 0)


def backward_kernel(
    ctx_size, tp_size,
    table_ref, q_ref, do_ref, fo_ref, kv_ref, w_ref,
    dq_ref, out_ref,
    qx, qs, dox, dos, kx, kt, vx, score, dkv,
    gathered, mate_sum, row_out, row_in, far_out, far_in, grad_ref, wall_ref, staged,
    gz_send, gz_recv, gy_send, gy_recv, gm_send, gm_recv,
    rm_send, rm_recv, ry_send, ry_recv, rz_send, rz_recv,
    wx_send, wx_recv, wm_send, wm_recv, own_sem, t_send, t_recv,
    stage_sem, bx_send, bx_recv, bz_send, bz_recv, by_send, by_recv, bm_send, bm_recv,
):
    tokens = q_ref.shape[0]
    total_rows = gathered.shape[0]
    far = ctx_size // 4
    me = lax.axis_index("ctx")
    tp = lax.axis_index("tp")
    hi, mid, core = me // 4, lax.rem(me // 2, 2), lax.rem(me, 2)

    def place(h, m, k):
        return h * 4 + m * 2 + k

    def around(step):
        return lax.rem(hi + step, far)

    def behind(step):
        return lax.rem(hi + far - step, far)

    def block(owner):
        return gathered.at[pl.ds(pl.multiple_of(owner * tokens, tokens), tokens), :]

    def send(src, dst, send_sem, recv_sem, axis, target):
        copy = pltpu.make_async_remote_copy(
            src_ref=src, dst_ref=dst, send_sem=send_sem, recv_sem=recv_sem,
            device_id={axis: target}, device_id_type=pl.DeviceIdType.MESH,
        )
        copy.start()
        return copy

    row_mate, core_mate = place(hi, 1 - mid, core), place(hi, mid, 1 - core)
    partners = [("ctx", place(around(step), mid, core)) for step in range(1, far)]
    partners += [("ctx", row_mate), ("ctx", core_mate)]
    partners += [("tp", lax.rem(tp + step, tp_size)) for step in range(1, tp_size)]
    features = w_ref.shape[0] // tp_size
    spread = spread_block(features, ctx_size)
    spread_rows = spread * ctx_size
    share = (features - spread_rows) // 2
    pieces = weight_pieces(share, wx_send.shape[1])
    piece_rows = share // pieces
    own_copy = pltpu.make_async_copy(
        w_ref.at[pl.ds(pl.multiple_of(tp * features, 16), features), :], wall_ref.at[0], own_sem
    )
    staging = []
    for step in range(1, tp_size):
        target = lax.rem(tp + step, tp_size) * features
        first = pl.multiple_of(target + me * spread, 16)
        staging.append(pltpu.make_async_copy(
            w_ref.at[pl.ds(first, spread), :], staged.at[step - 1, pl.ds(0, spread), :], stage_sem.at[step, 0]
        ))
        first = pl.multiple_of(target + spread_rows + core * share, 16)
        staging.append(pltpu.make_async_copy(
            w_ref.at[pl.ds(first, share), :], staged.at[step - 1, pl.ds(spread, share), :], stage_sem.at[step, 1]
        ))
    for copy in staging:
        copy.start()

    barrier = pltpu.get_barrier_semaphore()
    for axis, target in partners:
        pl.semaphore_signal(barrier, inc=1, device_id={axis: target}, device_id_type=pl.DeviceIdType.MESH)
    pl.semaphore_wait(barrier, len(partners))

    waits = []
    for step in range(1, far):
        waits.append(send(kv_ref, block(me), gz_send.at[step], gz_recv.at[step], "ctx", place(around(step), mid, core)))
    from_far = list(waits)
    from_row = [send(kv_ref, block(me), gy_send.at[0], gy_recv.at[0], "ctx", row_mate)]
    from_core = [send(kv_ref, block(me), gm_send.at[0, 0], gm_recv.at[0, 0], "ctx", core_mate)]

    own_copy.start()
    for copy in staging:
        copy.wait()

    def wall_piece(step, side, piece):
        first = pl.multiple_of(spread_rows + side * share + piece * piece_rows, 16)
        return wall_ref.at[step, pl.ds(first, piece_rows), :]

    def wall_block(step, owner):
        return wall_ref.at[step, pl.ds(pl.multiple_of(owner * spread, 16), spread), :]

    block_in = {}
    for step in range(1, tp_size):
        block_in[step] = send(
            staged.at[step - 1, pl.ds(0, spread), :], wall_block(step, me),
            bx_send.at[step], bx_recv.at[step], "tp", lax.rem(tp + step, tp_size),
        )
    weight_in = {}
    for piece in range(pieces):
        for step in range(1, tp_size):
            weight_in[step, piece] = send(
                staged.at[step - 1, pl.ds(spread + piece * piece_rows, piece_rows), :], wall_piece(step, core, piece),
                wx_send.at[step, piece], wx_recv.at[step, piece], "tp", lax.rem(tp + step, tp_size),
            )
    weight_mate, block_far, block_row, block_core = [], {}, {}, []

    def block_to_mates(step, hop):
        here = wall_block(step, place(behind(hop), mid, core))
        block_row[step, hop] = send(here, here, by_send.at[step, hop], by_recv.at[step, hop], "ctx", row_mate)
        block_core.append(send(here, here, bm_send.at[step, hop, 0], bm_recv.at[step, hop, 0], "ctx", core_mate))

    def spread_own_blocks():
        for step in range(1, tp_size):
            block_in[step].wait_recv()
            here = wall_block(step, me)
            for hop in range(1, far):
                block_far[step, hop] = send(
                    here, here, bz_send.at[step, hop], bz_recv.at[step, hop], "ctx", place(around(hop), mid, core)
                )
            block_to_mates(step, 0)

    def spread_far_block(hop):
        for step in range(1, tp_size):
            block_far[step, hop].wait_recv()
            block_to_mates(step, hop)

    def spread_row_block(hop):
        for step in range(1, tp_size):
            block_row[step, hop].wait_recv()
            here = wall_block(step, place(behind(hop), 1 - mid, core))
            block_core.append(
                send(here, here, bm_send.at[step, hop, 1], bm_recv.at[step, hop, 1], "ctx", core_mate)
            )

    tasks = [(spread_far_block, hop) for hop in range(1, far)]
    tasks.insert(1, (spread_row_block, 0))
    tasks += [(spread_row_block, hop) for hop in range(1, far)]
    points = 6

    def run_tasks(point):
        for index, (task, hop) in enumerate(tasks):
            if index * points // len(tasks) == point:
                task(hop)

    first_span = me * 2
    spread_queries(table_ref, first_span, 0, q_ref, do_ref, fo_ref, qx, qs, dox, dos)
    for step in range(1, far):
        from_far[step - 1].wait_recv()
        here = block(place(behind(step), mid, core))
        from_row.append(send(here, here, gy_send.at[step], gy_recv.at[step], "ctx", row_mate))
        from_core.append(send(here, here, gm_send.at[step, 0], gm_recv.at[step, 0], "ctx", core_mate))
    spread_queries(table_ref, first_span, 1, q_ref, do_ref, fo_ref, qx, qs, dox, dos)
    for step in range(far):
        from_row[step].wait_recv()
        here = block(place(behind(step), 1 - mid, core))
        from_core.append(send(here, here, gm_send.at[step, 1], gm_recv.at[step, 1], "ctx", core_mate))

    def take(owner, ref):
        first_row = pl.multiple_of(owner * tokens, tokens)
        spread_keys(table_ref, first_span, first_row, ref[...], kx, kt, vx)

    take(me, kv_ref)

    @pl.loop(1, 2 * far)
    def _(turn):
        owner = place(behind(turn // 2), lax.rem(mid + lax.rem(turn, 2), 2), core)
        take(owner, block(owner))

    for copy in from_core:
        copy.wait_recv()

    @pl.loop(0, 2 * far)
    def _(turn):
        owner = place(behind(turn // 2), lax.rem(mid + lax.rem(turn, 2), 2), 1 - core)
        take(owner, block(owner))

    for copy in from_far + from_row + from_core:
        copy.wait_send()

    def share_weights(piece):
        for step in range(1, tp_size):
            weight_in[step, piece].wait_recv()
            here = wall_piece(step, core, piece)
            weight_mate.append(
                send(here, here, wm_send.at[step, piece], wm_recv.at[step, piece], "ctx", core_mate)
            )

    chunk_rows = CHUNK_HEADS * tokens // 2
    chunk_count = qx.shape[0] // chunk_rows
    spread_own_blocks()

    def after_chunk(chunk):
        if chunk + 1 < chunk_count:
            run_tasks(2 * chunk)
            if chunk < pieces:
                share_weights(chunk)

    def mid_chunk(chunk):
        if 1 <= chunk and chunk + 1 < chunk_count:
            run_tasks(2 * chunk - 1)

    def turn_place(turn):
        return around(turn % far + 1), (1 - mid if turn < far else mid)

    def tile_order(turn):
        h, m = turn_place(turn)
        return h * 2 + m

    def part(turn, k):
        h, m = turn_place(turn)
        return pl.ds(pl.multiple_of(place(h, m, k) * tokens, tokens), tokens)

    to_core, to_row, to_far = [], [], []

    def pass_on(turn):
        to_core[turn].wait_recv()
        total = dkv[part(turn, core), :] + mate_sum[turn]
        step = turn % far
        if turn < far:
            row_out[step] = total.astype(jnp.bfloat16)
            to_row.append(send(row_out.at[step], row_in.at[step], ry_send.at[step], ry_recv.at[step], "ctx", row_mate))
            return
        to_row[step].wait_recv()
        total = total + row_in[step].astype(jnp.float32)
        if step + 1 < far:
            far_out[step] = total.astype(jnp.bfloat16)
            h, _ = turn_place(turn)
            to_far.append(
                send(far_out.at[step], far_in.at[step], rz_send.at[step], rz_recv.at[step], "ctx", place(h, mid, core))
            )
            return
        for copy in to_far:
            copy.wait_recv()
        for step in range(far - 1):
            total = total + far_in[step].astype(jnp.float32)
        grad_ref[0] = total.astype(jnp.bfloat16)

    lag = 3

    def after_tile(turn):
        to_core.append(
            send(dkv.at[part(turn, 1 - core), :], mate_sum.at[turn], rm_send.at[turn], rm_recv.at[turn], "ctx", core_mate)
        )
        if turn >= lag:
            pass_on(turn - lag)

    attention(
        chunk_count, chunk_rows, total_rows, tokens // 2, kx, kt, vx, qx, qs, dox, dos, score, dkv, dq_ref,
        mid_chunk, after_chunk, tile_order, after_tile,
    )
    for turn in range(2 * far - lag, 2 * far):
        if turn + 1 == 2 * far:
            run_tasks(points - 1)
            for piece in range(chunk_count - 1, pieces):
                share_weights(piece)
        pass_on(turn)
    last = []
    for step in range(1, tp_size):
        last.append(
            send(
                grad_ref.at[0], grad_ref.at[step],
                t_send.at[step], t_recv.at[step], "tp", lax.rem(tp + step, tp_size),
            )
        )
    for copy in last + weight_mate + block_core:
        copy.wait_recv()
    own_copy.wait()
    grad = jnp.concatenate([grad_ref[step] for step in range(tp_size)], axis=1)
    for first, count in feature_chunks(features):
        at = pl.ds(first, count)
        weights = jnp.concatenate([wall_ref[step, at, :] for step in range(tp_size)], axis=1)
        out_ref[:, at] = dot(grad, weights, NT).astype(jnp.bfloat16)
    for copy in to_core + to_row + to_far + last + weight_mate + block_core:
        copy.wait_send()
    for copies in (weight_in, block_in, block_far, block_row):
        for copy in copies.values():
            copy.wait_send()


def spread_block(features, ctx_size):
    return 16 * (features * 11 // (20 * 16 * ctx_size))


def feature_chunks(features):
    if features % 128:
        return [(0, features)]
    step = 1024
    return [(first, min(step, features - first)) for first in range(0, features, step)]


def scratch(tokens, heads, features, ctx_size, tp_size):
    total_rows = tokens * ctx_size
    rows = tokens * heads
    chunk_rows = CHUNK_HEADS * tokens // 2
    far = ctx_size // 4
    block = (tokens, 2 * HEAD)
    spread = spread_block(features, ctx_size)
    share = (features - spread * ctx_size) // 2
    sems = pltpu.SemaphoreType.DMA
    return [
        pltpu.VMEM((rows, 4 * HEAD), jnp.bfloat16),
        pltpu.VMEM((rows, 2 * HEAD), jnp.bfloat16),
        pltpu.VMEM((rows, 2 * HEAD), jnp.bfloat16),
        pltpu.VMEM((rows, 2 * HEAD), jnp.bfloat16),
        pltpu.VMEM((2, total_rows, 4 * HEAD), jnp.bfloat16),
        pltpu.VMEM((HEAD, total_rows), jnp.bfloat16),
        pltpu.VMEM((total_rows, 2 * HEAD), jnp.bfloat16),
        pltpu.VMEM((2, total_rows, chunk_rows), jnp.float32),
        pltpu.VMEM((total_rows, 2 * HEAD), jnp.float32),
        pltpu.VMEM((total_rows, 2 * HEAD), jnp.bfloat16),
        pltpu.VMEM((2 * far,) + block, jnp.float32),
        pltpu.VMEM((far,) + block, jnp.bfloat16),
        pltpu.VMEM((far,) + block, jnp.bfloat16),
        pltpu.VMEM((far,) + block, jnp.bfloat16),
        pltpu.VMEM((far,) + block, jnp.bfloat16),
        pltpu.VMEM((tp_size,) + block, jnp.bfloat16),
        pltpu.VMEM((tp_size, features, 2 * HEAD), jnp.bfloat16),
        pltpu.VMEM((tp_size - 1, spread + share, 2 * HEAD), jnp.bfloat16),
        sems((far,)), sems((far,)), sems((far,)), sems((far,)), sems((far, 2)), sems((far, 2)),
        sems((2 * far,)), sems((2 * far,)), sems((far,)), sems((far,)), sems((far,)), sems((far,)),
        sems((tp_size, 4)), sems((tp_size, 4)), sems((tp_size, 4)), sems((tp_size, 4)), sems(()),
        sems((tp_size,)), sems((tp_size,)),
        sems((tp_size, 2)), sems((tp_size,)), sems((tp_size,)), sems((tp_size, far)), sems((tp_size, far)),
        sems((tp_size, far)), sems((tp_size, far)), sems((tp_size, far, 2)), sems((tp_size, far, 2)),
    ]


def on_device(queries, keys_values, forward_out, out_grad, kv_weight, span_table):
    tokens = queries.shape[0]
    heads = queries.shape[1] // HEAD
    tp_size = lax.axis_size("tp")
    ctx_size = lax.axis_size("ctx")
    features = kv_weight.shape[0] // tp_size
    vmem = pl.BlockSpec(memory_space=pltpu.VMEM)
    anywhere = pl.BlockSpec(memory_space=pl.ANY)
    return pl.pallas_call(
        functools.partial(backward_kernel, ctx_size, tp_size),
        out_shape=(
            jax.ShapeDtypeStruct(queries.shape, jnp.bfloat16),
            jax.ShapeDtypeStruct((tokens, features), jnp.bfloat16),
        ),
        in_specs=[pl.BlockSpec(memory_space=pltpu.SMEM)] + [vmem] * 4 + [anywhere],
        out_specs=(vmem, vmem),
        scratch_shapes=scratch(tokens, heads, features, ctx_size, tp_size),
        compiler_params=pltpu.CompilerParams(
            vmem_limit_bytes=50 * 2**20, collective_id=0, has_side_effects=True
        ),
    )(span_table, queries, out_grad, forward_out, keys_values, kv_weight)


def solution(mesh):
    placed = (P("ctx", "tp"), P("ctx", "tp"), P("ctx", "tp"), P("ctx", "tp"), P(None, "tp"), P())
    return jax.shard_map(
        on_device,
        mesh=mesh,
        in_specs=placed,
        out_specs=(P("ctx", "tp"), P("ctx", "tp")),
        check_vma=False,
    )
```
